128 devices in a mesh: cfg: 2 (over x_lo), th: 2 (over core), tw: 4 (over z), hd: 8 (over x_hi, y).
Axes of the slice: x: 4 (x_hi: 2, x_lo: 2; x = x_hi * 2 + x_lo), y: 4, z: 4, core: 2. Of those that a mesh axis runs over, the one named last changes fastest.
Arguments:
- video: bfloat16 [2, 6, 32, 64, 3072], P('cfg', None, 'th', 'tw'), may hold values from -6 to 6
- text_states: bfloat16 [2, 256, 3072], P('cfg'), may hold values from -6 to 6
- text_count: int32 [2], P('cfg'), may hold values from 32 to 256, as said below
- guidance: float32 [1], replicated, may hold values from 4 to 7
- window_offsets: int32 [24, 2], P('hd'), may hold values from -1 to 1
- w_qkv: bfloat16 [3072, 3, 3072], P(('cfg', 'th', 'tw'), None, 'hd'), may hold values from -0.109375 to 0.109375
- q_gain: float32 [24, 128], P('hd'), may hold values from 1 to 2.5
- k_gain: float32 [24, 128], P('hd'), may hold values from 1 to 2.5
- w_out: bfloat16 [3072, 3072], P('hd', ('cfg', 'th', 'tw')), may hold values from -0.109375 to 0.109375
Outputs:
- guided: bfloat16 [6, 32, 64, 3072], P(None, 'th', 'tw', ('cfg', 'hd'))
The draws below stay inside these ranges and needn't reach their ends.
Inputs may be any that keep to these rules, and one draw needn't show every extreme that they name: `text_count`: one of the two branches has all 256 text tokens valid.
All inputs are finite; a program needn't handle non-finite values.
Results may differ from the reference program's by a relative error of at most 0.0085.
The reference program's roundings to bfloat16 on the way count: a program that leaves them out, or rounds other values in their place, can miss the bound.
Values may be sent and summed in bfloat16 or wider, within the bound.
A program may use at most 128 MiB of HBM per device.

```python
import math
import jax
import jax.numpy as jnp
from jax import lax

D = 3072
HEADS = 24
HD = 128
F = 6
TXT = 256
H = 32
W = 64


def draw_text_count(key, part):
    key = jax.random.fold_in(key, 7)
    first_key, second_key = jax.random.split(key)
    other_count = jax.random.randint(first_key, (), TXT // 8, TXT + 1)
    flipped = jax.random.randint(second_key, (), 0, 2)
    full_count = jnp.full((), TXT, jnp.int32)
    ordered = jnp.stack([full_count, other_count.astype(jnp.int32)])
    swapped = jnp.stack([other_count.astype(jnp.int32), full_count])
    return jnp.where(flipped == 0, ordered, swapped).astype(jnp.int32)


def place_ends(values, own_key, low, top_value):
    longest = values.shape.index(max(values.shape))
    spots = []
    for shift in (0, 1):
        where = [jax.random.randint(jax.random.fold_in(own_key, axis), (), 0, length) for axis, length in enumerate(values.shape)]
        where[longest] = (where[longest] + shift) % values.shape[longest]
        spots.append(tuple(where))
    return values.at[spots[0]].set(low).at[spots[1]].set(top_value)


def block_levels(own_key, extent, shards, least, high):
    def one(dim, shards_of):
        steps = jax.random.uniform(jax.random.fold_in(jax.random.fold_in(own_key, 6), dim), (shards_of,), jnp.float32, least / len(shards), high / len(shards))
        return jnp.repeat(jnp.exp(steps), extent[dim] // shards_of).reshape((-1,) + (1,) * (len(extent) - dim - 1))

    loudness = one(*shards[0])
    for cut in shards[1:]:
        loudness = loudness * one(*cut)
    return loudness


def gaussian(rng, dims, deviation, bound, cuts=(), held_as=jnp.bfloat16):
    array = deviation * jax.random.normal(rng, dims, jnp.float32)
    if cuts:
        array = array * block_levels(rng, dims, cuts, -0.22, 0.18)
    return jnp.clip(array, -bound, bound).astype(held_as)


def setup_inputs(seed: int = 0) -> dict:
    splits = jax.random.split(jax.random.key(seed), 10)
    return {
        "video": gaussian(splits[0], (2, F, H, W, D), 1.0, 6.0, ((0, 2), (2, 2), (3, 4))),
        "text_states": gaussian(splits[1], (2, TXT, D), 1.0, 6.0, ((0, 2),)),
        "text_count": draw_text_count(jax.random.fold_in(splits[9], 71), 0),
        "guidance": jnp.clip(jax.random.uniform(splits[3], (1,), jnp.float32, 4.0, 7.0), 4.0, 7.0),
        "window_offsets": place_ends(jax.random.randint(splits[4], (HEADS, 2), -1, 2), jax.random.fold_in(splits[4], 1), -1, 1).astype(jnp.int32),
        "w_qkv": gaussian(splits[5], (D, 3, HEADS * HD), D ** -0.5, 0.109375, ((0, 16), (2, 8))),
        "q_gain": jnp.clip(jnp.exp(math.log(2.5) - 0.916290732 * jax.random.uniform(splits[6], (HEADS, HD), jnp.float32) ** block_levels(splits[6], (HEADS, HD), ((0, 8),), -0.2, 0.2)), 1.0, 2.5),
        "k_gain": jnp.clip(jnp.exp(math.log(2.5) - 0.916290732 * jax.random.uniform(splits[7], (HEADS, HD), jnp.float32) ** block_levels(splits[7], (HEADS, HD), ((0, 8),), -0.2, 0.2)), 1.0, 2.5),
        "w_out": gaussian(splits[8], (HEADS * HD, D), (HEADS * HD) ** -0.5, 0.109375, ((0, 8), (1, 16))),
    }


def scaled_norm(values, gain):
    mean_square = lax.optimization_barrier(jnp.mean(values * values, axis=-1, keepdims=True))
    return values * lax.rsqrt(mean_square + 1e-06) * gain

def attend(queries, keys, values, text_keys, text_values, count):
    factor = 1.0 / queries.shape[-1] ** 0.5
    scores = jnp.dot(queries, keys.T, preferred_element_type=jnp.float32) * factor
    text_scores = jnp.dot(queries, text_keys.T, preferred_element_type=jnp.float32) * factor
    valid = jnp.arange(text_keys.shape[0], dtype=jnp.int32) < count
    expo = jnp.exp(scores)
    text_expo = jnp.where(valid[None, :], jnp.exp(text_scores), 0.0)
    total = lax.optimization_barrier(jnp.sum(expo, axis=1, keepdims=True)) + lax.optimization_barrier(jnp.sum(text_expo, axis=1, keepdims=True))
    probs = (expo / total).astype(jnp.bfloat16)
    text_probs = (text_expo / total).astype(jnp.bfloat16)
    result = jnp.dot(probs, values, preferred_element_type=jnp.float32)
    result = result + jnp.dot(text_probs, text_values, preferred_element_type=jnp.float32)
    return result.astype(jnp.bfloat16)

def branch_output(frames, text_rows, count, window_offsets, w_qkv, q_gain, k_gain, w_out):
    n_frames, rows_total, cols_total, model_width = frames.shape
    head_count, head_size = q_gain.shape
    tile_rows = rows_total // 8
    tile_cols = cols_total // 8
    flat = frames.reshape(-1, model_width)
    proj = jnp.dot(flat, w_qkv.reshape(model_width, -1), preferred_element_type=jnp.float32)
    proj = proj.reshape(n_frames, rows_total, cols_total, 3, head_count, head_size)
    queries = scaled_norm(proj[:, :, :, 0], q_gain).astype(jnp.bfloat16)
    keys = scaled_norm(proj[:, :, :, 1], k_gain).astype(jnp.bfloat16)
    values = proj[:, :, :, 2].astype(jnp.bfloat16)
    text_proj = jnp.dot(text_rows, w_qkv[:, 1:].reshape(model_width, -1), preferred_element_type=jnp.float32)
    text_proj = text_proj.reshape(-1, 2, head_count, head_size)
    text_keys = scaled_norm(text_proj[:, 0], k_gain).astype(jnp.bfloat16)
    text_values = text_proj[:, 1].astype(jnp.bfloat16)

    def head_output(head):
        head_q = lax.dynamic_index_in_dim(queries, head, 3, False)
        head_k = lax.dynamic_index_in_dim(keys, head, 3, False)
        head_v = lax.dynamic_index_in_dim(values, head, 3, False)
        head_tk = lax.dynamic_index_in_dim(text_keys, head, 1, False)
        head_tv = lax.dynamic_index_in_dim(text_values, head, 1, False)
        offset = lax.dynamic_index_in_dim(window_offsets, head, 0, False)

        def tile_output(tile_index):
            row_tile = (tile_index // tile_cols).astype(jnp.int32)
            col_tile = (tile_index % tile_cols).astype(jnp.int32)
            center_row = jnp.clip(row_tile + offset[0], 1, tile_rows - 2).astype(jnp.int32)
            center_col = jnp.clip(col_tile + offset[1], 1, tile_cols - 2).astype(jnp.int32)
            zero = jnp.zeros((), jnp.int32)
            tile_q = lax.dynamic_slice(head_q, (zero, row_tile * 8, col_tile * 8, zero), (n_frames, 8, 8, head_size))
            start_k = (zero, (center_row - 1) * 8, (center_col - 1) * 8, zero)
            tile_k = lax.dynamic_slice(head_k, start_k, (n_frames, 24, 24, head_size))
            tile_v = lax.dynamic_slice(head_v, start_k, (n_frames, 24, 24, head_size))
            return attend(tile_q.reshape(-1, head_size), tile_k.reshape(-1, head_size), tile_v.reshape(-1, head_size), head_tk, head_tv, count)
        return jax.vmap(tile_output)(jnp.arange(tile_rows * tile_cols, dtype=jnp.int32))
    outputs = lax.map(head_output, jnp.arange(head_count, dtype=jnp.int32))
    outputs = outputs.reshape(head_count, tile_rows, tile_cols, n_frames, 8, 8, head_size)
    outputs = jnp.transpose(outputs, (3, 1, 4, 2, 5, 0, 6)).reshape(-1, head_count * head_size)
    return jnp.dot(outputs, w_out, preferred_element_type=jnp.float32)

def reference(video, text_states, text_count, guidance, window_offsets, w_qkv, q_gain, k_gain, w_out):
    first = branch_output(video[0], text_states[0], text_count[0], window_offsets, w_qkv, q_gain, k_gain, w_out)
    second = branch_output(video[1], text_states[1], text_count[1], window_offsets, w_qkv, q_gain, k_gain, w_out)
    scale_value = guidance[0]
    combined = scale_value * first + (1.0 - scale_value) * second
    return combined.reshape(video.shape[1:]).astype(jnp.bfloat16)
```

```python
import functools
import math

import jax
import jax.numpy as jnp
from jax import lax
from jax.experimental import pallas as pl
from jax.experimental.pallas import tpu as pltpu
from jax.sharding import PartitionSpec as P

MESH = pl.DeviceIdType.MESH
BF = jnp.bfloat16
F32 = jnp.float32
VMEM = pl.BlockSpec(memory_space=pltpu.VMEM)
SMEM = pl.BlockSpec(memory_space=pltpu.SMEM)
ANY = pl.BlockSpec(memory_space=pl.ANY)
LIMIT = 62 << 20
TILE = 384
TOK = 1536


def place():
    c, t, w, h = (lax.axis_index(a) for a in ("cfg", "th", "tw", "hd"))
    return c, t, w, h // 4, lax.rem(h, 4)


def partners():
    c, t, w, x, y = place()
    return {
        "left": {"tw": lax.rem(w + 3, 4)},
        "right": {"tw": lax.rem(w + 1, 4)},
        "core": {"th": 1 - t},
        "xl": {"cfg": 1 - c},
        "xh": {"hd": (1 - x) * 4 + y},
        "xd": {"cfg": 1 - c, "hd": (1 - x) * 4 + y},
        "up": {"hd": x * 4 + lax.rem(y + 1, 4)},
        "down": {"hd": x * 4 + lax.rem(y + 3, 4)},
    }


def greet(names):
    to = partners()
    barrier = pltpu.get_barrier_semaphore()
    for name in names:
        pl.semaphore_signal(barrier, inc=1, device_id=to[name], device_id_type=MESH)
    pl.semaphore_wait(barrier, len(names))


class Mail:
    def __init__(self, send, recv):
        self.send, self.recv, self.n, self.all = send, recv, 0, []
        self.to = partners()

    def copy(self, src, dst, name):
        k = self.n
        self.n += 1
        cp = pltpu.make_async_remote_copy(
            src_ref=src,
            dst_ref=dst,
            send_sem=self.send.at[k],
            recv_sem=self.recv.at[k],
            device_id=self.to[name],
            device_id_type=MESH,
        )
        self.all.append(cp)
        return cp

    def post(self, src, dst, name):
        cp = self.copy(src, dst, name)
        cp.start()
        return cp

    def close(self):
        for cp in self.all:
            cp.wait_send()


def normed(v, gain):
    ms = jnp.mean(v * v, axis=-1, keepdims=True)
    return v * lax.rsqrt(ms + 1e-06) * gain


GROUP_PIECES = (((1, 0), (2, 0)), ((1, 1), (2, 1)), ((1, 2), (2, 2)), ((0, 0), (0, 1)), ((0, 2),))
N_GROUPS = len(GROUP_PIECES)
N_MAIL1 = N_GROUPS * 16 + 8


def project_kernel(
    video, wq, wo, text, qg, kg, q_out, kv_out, tkv_out, wo_out, xv, tv, wv0, wv1, wv2, wv3, wv4, wov, lsem, ssem, rsem
):
    c, t, w, x, y = place()
    wv = (wv0, wv1, wv2, wv3, wv4)
    half = 768
    loads = [
        pltpu.make_async_copy(video.at[pl.ds(i * half, half)], xv.at[pl.ds(i * half, half)], lsem.at[i])
        for i in range(2)
    ]
    loads.append(pltpu.make_async_copy(text, tv, lsem.at[2]))

    def rows(cc, tt, ww):
        return pl.ds(pl.multiple_of((cc * 8 + tt * 4 + ww) * 192, 64), 192)

    own = rows(c, t, w)
    w_loads = []
    n = 3
    for g, pieces in enumerate(GROUP_PIECES):
        for k, (part, h) in enumerate(pieces):
            cp = pltpu.make_async_copy(
                wq.at[:, pl.ds(part * 384 + h * 128, 128)], wv[g].at[own, pl.ds(k * 128, 128)], lsem.at[n]
            )
            n += 1
            cp.start()
            w_loads.append(cp)
    wo_load = pltpu.make_async_copy(wo, wov.at[w], lsem.at[n])
    wo_load.start()
    for cp in loads:
        cp.start()
    greet(("left", "right", "xl", "core"))
    for cp in w_loads:
        cp.wait()
    mail = Mail(ssem, rsem)
    wl, wr, w2 = lax.rem(w + 3, 4), lax.rem(w + 1, 4), lax.rem(w + 2, 4)
    state = [None] * N_GROUPS

    def half_rows(cc, tt, ww, k):
        return pl.ds(pl.multiple_of((cc * 8 + tt * 4 + ww) * 192 + k * 96, 32), 96)

    def start_own(g):
        ref = wv[g]
        s = {}
        for name in ("left", "right", "xl", "core"):
            s[name] = mail.post(ref.at[own], ref.at[own], name)
        state[g] = s

    def z_events(g):
        ref, s = wv[g], state[g]
        s["right"].wait_recv()
        r = half_rows(c, t, wl, 0)
        s["r2"] = mail.post(ref.at[r], ref.at[r], "right")
        r = rows(c, t, wl)
        s["x1"] = mail.post(ref.at[r], ref.at[r], "xl")
        s["c1"] = mail.post(ref.at[r], ref.at[r], "core")
        s["left"].wait_recv()
        r = half_rows(c, t, wr, 1)
        s["l2"] = mail.post(ref.at[r], ref.at[r], "left")
        r = rows(c, t, wr)
        s["x2"] = mail.post(ref.at[r], ref.at[r], "xl")
        s["c2"] = mail.post(ref.at[r], ref.at[r], "core")
        s["r2"].wait_recv()
        s["l2"].wait_recv()
        r = rows(c, t, w2)
        s["x3"] = mail.post(ref.at[r], ref.at[r], "xl")
        s["c3"] = mail.post(ref.at[r], ref.at[r], "core")

    def x_events(g):
        ref, s = wv[g], state[g]
        for k, (key, ww) in enumerate((("xl", w), ("x1", wl), ("x2", wr), ("x3", w2))):
            s[key].wait_recv()
            r = rows(1 - c, t, ww)
            s["d%d" % k] = mail.post(ref.at[r], ref.at[r], "core")
        for key in ("core", "c1", "c2", "c3", "d0", "d1", "d2", "d3"):
            s[key].wait_recv()

    def multiply(g):
        ref, pieces = wv[g], GROUP_PIECES[g]

        def step(mc, carry):
            acc = jnp.dot(
                xv[pl.ds(pl.multiple_of(mc * half, half), half), :], ref[...], preferred_element_type=F32
            )
            for k, (part, h) in enumerate(pieces):
                v = acc[:, k * 128 : (k + 1) * 128]
                if part < 2:
                    v = normed(v, (qg if part == 0 else kg)[h : h + 1, :])
                v = v.reshape(3, 2, 8, 2, 8, 128)
                for i in range(2):
                    for j in range(2):
                        tile = v[:, i, :, j].reshape(192, 128).astype(BF)
                        if part == 0:
                            q_out[h, i * 2 + j, pl.ds(pl.multiple_of(mc * 192, 64), 192), :] = tile
                        else:
                            kv_out[h, j, part - 1, i, pl.ds(pl.multiple_of(mc * 192, 64), 192), :] = tile
            return carry

        lax.fori_loop(0, 2, step, 0)
        if pieces[0][0] == 1:
            h = pieces[0][1]
            acc = jnp.dot(tv[...], ref[...], preferred_element_type=F32)
            tkv_out[h, 0] = normed(acc[:, :128], kg[h : h + 1, :]).astype(BF)
            tkv_out[h, 1] = acc[:, 128:].astype(BF)

    start_own(0)
    start_own(1)
    z_events(0)
    for g in range(N_GROUPS):
        if g + 2 < N_GROUPS:
            start_own(g + 2)
        if g + 1 < N_GROUPS:
            z_events(g + 1)
        if g == 2:
            wo_load.wait()
            o_left = mail.post(wov.at[w], wov.at[w], "left")
            o_right = mail.post(wov.at[w], wov.at[w], "right")
        if g == 3:
            o_right.wait_recv()
            o_r2 = mail.post(wov.at[wl, pl.ds(0, 96)], wov.at[wl, pl.ds(0, 96)], "right")
            o_left.wait_recv()
            o_l2 = mail.post(wov.at[wr, pl.ds(96, 96)], wov.at[wr, pl.ds(96, 96)], "left")
        x_events(g)
        if g == 0:
            for cp in loads:
                cp.wait()
        multiply(g)
    o_r2.wait_recv()
    o_l2.wait_recv()
    wo_out[...] = wov[...]
    mail.close()


def project(video, wq, wo, text, qg, kg):
    return pl.pallas_call(
        project_kernel,
        out_shape=(
            jax.ShapeDtypeStruct((3, 4, TILE, 128), BF),
            jax.ShapeDtypeStruct((3, 2, 2, 2, TILE, 128), BF),
            jax.ShapeDtypeStruct((3, 2, 256, 128), BF),
            jax.ShapeDtypeStruct((4, 192, 384), BF),
        ),
        in_specs=[ANY, ANY, ANY, ANY, VMEM, VMEM],
        out_specs=(VMEM, VMEM, VMEM, VMEM),
        scratch_shapes=[
            pltpu.VMEM((TOK, 3072), BF),
            pltpu.VMEM((256, 3072), BF),
            pltpu.VMEM((3072, 256), BF),
            pltpu.VMEM((3072, 256), BF),
            pltpu.VMEM((3072, 256), BF),
            pltpu.VMEM((3072, 256), BF),
            pltpu.VMEM((3072, 128), BF),
            pltpu.VMEM((4, 192, 384), BF),
            pltpu.SemaphoreType.DMA((16,)),
            pltpu.SemaphoreType.DMA((N_MAIL1,)),
            pltpu.SemaphoreType.DMA((N_MAIL1,)),
        ],
        compiler_params=pltpu.CompilerParams(collective_id=0, has_side_effects=True, vmem_limit_bytes=LIMIT),
    )(video, wq, wo, text, qg, kg)


SCALE = math.log2(math.e) / math.sqrt(128.0)


def attend_tile(q, kvb, p0, r0, tk, tv, count):
    def weights(keys):
        s = lax.dot_general(q, keys, (((1,), (1,)), ((), ())), preferred_element_type=F32)
        return jnp.exp2(s * SCALE)

    p = weights(tk)
    valid = lax.broadcasted_iota(jnp.int32, p.shape, 1) < count
    p = jnp.where(valid, p, 0.0)
    den = jnp.sum(p, axis=1, keepdims=True)
    acc = jnp.dot(p.astype(BF), tv, preferred_element_type=F32)
    span = pl.ds(r0, 3)
    for d in range(3):
        p = weights(kvb[p0 + d, 0, span].reshape(3 * TILE, 128))
        den = den + jnp.sum(p, axis=1, keepdims=True)
        acc = acc + jnp.dot(p.astype(BF), kvb[p0 + d, 1, span].reshape(3 * TILE, 128), preferred_element_type=F32)
    return (acc / den).astype(BF)


N_MAIL2 = 3 * 9 + 8


def attend_kernel(q, kv, tkv, wo, off, cnt, att, wt, kvb0, kvb1, kvb2, lsem, ssem, rsem):
    c, t, w, x, y = place()
    kvb = (kvb0, kvb1, kvb2)
    mine = pl.ds(2 * t, 2)
    lanes = pl.ds(pl.multiple_of(x * 384, 128), 384)
    local = [pltpu.make_async_copy(kv.at[h], kvb[h].at[pl.ds(2, 2), :, mine], lsem.at[h]) for h in range(3)]
    local.append(pltpu.make_async_copy(wo, wt.at[:, c, t, :, lanes], lsem.at[3]))
    for cp in local:
        cp.start()
    greet(("left", "right", "core", "xl", "xh", "xd"))
    mail = Mail(ssem, rsem)
    halo = []
    for h in range(3):
        b = kvb[h]
        halo.append(
            (
                mail.post(kv.at[h, 0], b.at[4, :, mine], "left"),
                mail.post(kv.at[h, 1], b.at[1, :, mine], "right"),
                mail.post(kv.at[h, 1], b.at[5, :, mine], "left"),
                mail.post(kv.at[h, 0], b.at[0, :, mine], "right"),
                mail.post(kv.at[h], b.at[pl.ds(2, 2), :, mine], "core"),
            )
        )
        if h == 0:
            wo_own = mail.post(wo, wt.at[:, c, t, :, lanes], "core")
            wo_x = [mail.post(wo, wt.at[:, c, t, :, lanes], name) for name in ("xl", "xh", "xd")]

    count = cnt[0]
    for h in range(3):
        b = kvb[h]
        relayed = []
        for k, p in enumerate((4, 1, 5, 0)):
            halo[h][k].wait_recv()
            relayed.append(mail.post(b.at[p, :, mine], b.at[p, :, mine], "core"))
        if h == 1:
            wo_core = []
            for cp, (cc, xx) in zip(wo_x, ((1 - c, x), (c, 1 - x), (1 - c, 1 - x))):
                cp.wait_recv()
                at = wt.at[:, cc, t, :, pl.ds(pl.multiple_of(xx * 384, 128), 384)]
                wo_core.append(mail.post(at, at, "core"))
        halo[h][4].wait_recv()
        for cp in relayed:
            cp.wait_recv()
        local[h].wait()

        def tile(k, carry):
            i, j = k // 2, lax.rem(k, 2)
            row = jnp.clip(2 * t + i + off[h, 0], 1, 2) - 1
            col = jnp.clip(2 * w + j + off[h, 1], 1, 6) + 1 - 2 * w
            att[k, :, h * 128 : (h + 1) * 128] = attend_tile(q[h, k], b, col, row, tkv[h, 0], tkv[h, 1], count)
            return carry

        lax.fori_loop(0, 4, tile, 0)
    local[3].wait()
    wo_own.wait_recv()
    for cp in wo_core:
        cp.wait_recv()
    mail.close()


def attention(q, kv, tkv, wo, off, cnt):
    return pl.pallas_call(
        attend_kernel,
        out_shape=(
            jax.ShapeDtypeStruct((4, TILE, 384), BF),
            jax.ShapeDtypeStruct((4, 2, 2, 192, 768), BF),
        ),
        in_specs=[VMEM, VMEM, VMEM, VMEM, SMEM, SMEM],
        out_specs=(VMEM, VMEM),
        scratch_shapes=[
            pltpu.VMEM((6, 2, 4, TILE, 128), BF),
            pltpu.VMEM((6, 2, 4, TILE, 128), BF),
            pltpu.VMEM((6, 2, 4, TILE, 128), BF),
            pltpu.SemaphoreType.DMA((4,)),
            pltpu.SemaphoreType.DMA((N_MAIL2,)),
            pltpu.SemaphoreType.DMA((N_MAIL2,)),
        ],
        compiler_params=pltpu.CompilerParams(collective_id=1, has_side_effects=True, vmem_limit_bytes=LIMIT),
    )(q, kv, tkv, wo, off, cnt)


def output_kernel(att, wt, guide, out, box, comb, s1, sent, got, mid, ends, lsem, ssem, rsem):
    c, t, w, x, y = place()
    greet(("xl", "xh", "xd", "up", "down"))
    mail = Mail(ssem, rsem)
    spot = c * 2 + x
    peers = (("xl", 1 - c, x), ("xh", c, 1 - x), ("xd", 1 - c, 1 - x))
    keep = pltpu.make_async_copy(att.at[spot], box.at[spot], lsem.at[0])
    keep.start()
    ins = [mail.post(att.at[cc * 2 + xx], box.at[spot], name) for name, cc, xx in peers]
    keep.wait()
    for cp in ins:
        cp.wait_recv()
    g = guide[0]
    for xx in range(2):
        mixed = g * box[xx].astype(F32) + (1.0 - g) * box[2 + xx].astype(F32)
        comb[:, xx * 384 : (xx + 1) * 384] = mixed.astype(BF)

    def term(yy, half):
        a = comb[...]
        parts = wt[yy, half].reshape(384, 768)
        return lax.dot_general(a, parts, (((1,), (1,)), ((), ())), preferred_element_type=F32)

    far, up, down = lax.rem(y + 2, 4), lax.rem(y + 1, 4), lax.rem(y + 3, 4)
    sent[0] = term(far, 0).astype(BF)
    a1 = mail.post(sent.at[0], s1.at[0], "up")
    sent[1] = term(far, 1).astype(BF)
    a2 = mail.post(sent.at[1], s1.at[1], "down")
    sent[2] = term(up, 1).astype(BF)
    b1 = mail.post(sent.at[2], got.at[0], "up")
    sent[3] = term(down, 0).astype(BF)
    b2 = mail.post(sent.at[3], got.at[1], "down")
    t_up = term(up, 0)
    a1.wait_recv()
    sent[4] = (t_up + s1[0].astype(F32)).astype(BF)
    b3 = mail.post(sent.at[4], got.at[2], "up")
    t_down = term(down, 1)
    a2.wait_recv()
    sent[5] = (t_down + s1[1].astype(F32)).astype(BF)
    b4 = mail.post(sent.at[5], got.at[3], "down")
    own0 = term(y, 0)
    own1 = term(y, 1)
    b2.wait_recv()
    b3.wait_recv()
    total0 = own0 + got[1].astype(F32) + got[2].astype(F32)
    b1.wait_recv()
    b4.wait_recv()
    total1 = own1 + got[0].astype(F32) + got[3].astype(F32)
    for k in range(2):
        mid[0, k] = total0[:, k * 192 : (k + 1) * 192].astype(BF)
        mid[1, k] = total1[:, k * 192 : (k + 1) * 192].astype(BF)
    keep = pltpu.make_async_copy(mid.at[c, x], ends.at[spot], lsem.at[1])
    keep.start()
    outs = [mail.post(mid.at[cc, xx], ends.at[spot], name) for name, cc, xx in peers]
    keep.wait()
    for cp in outs:
        cp.wait_recv()
    for i in range(2):
        sides = [ends[i * 2 + j].astype(F32).reshape(6, 8, 8, 192) for j in range(2)]
        out[:, i * 8 : (i + 1) * 8] = jnp.concatenate(sides, axis=2).astype(BF)
    mail.close()


def finish(att, wt, guide):
    return pl.pallas_call(
        output_kernel,
        out_shape=jax.ShapeDtypeStruct((6, 16, 16, 192), BF),
        in_specs=[VMEM, VMEM, SMEM],
        out_specs=VMEM,
        scratch_shapes=[
            pltpu.VMEM((4, TILE, 384), BF),
            pltpu.VMEM((TILE, 768), BF),
            pltpu.VMEM((2, TILE, 384), BF),
            pltpu.VMEM((6, TILE, 384), BF),
            pltpu.VMEM((4, TILE, 384), BF),
            pltpu.VMEM((2, 2, TILE, 192), BF),
            pltpu.VMEM((4, TILE, 192), BF),
            pltpu.SemaphoreType.DMA((2,)),
            pltpu.SemaphoreType.DMA((12,)),
            pltpu.SemaphoreType.DMA((12,)),
        ],
        compiler_params=pltpu.CompilerParams(collective_id=2, has_side_effects=True, vmem_limit_bytes=LIMIT),
    )(att, wt, guide)


def body(video, text_states, text_count, guidance, window_offsets, w_qkv, q_gain, k_gain, w_out):
    q, kv, tkv, wo = project(
        video.reshape(TOK, 3072), w_qkv.reshape(192, 1152), w_out.T, text_states[0], q_gain, k_gain
    )
    att, wt = attention(q, kv, tkv, wo, window_offsets, text_count)
    return finish(att, wt, guidance)


def solution(mesh):
    return jax.shard_map(
        body,
        mesh=mesh,
        in_specs=(
            P("cfg", None, "th", "tw", None),
            P("cfg", None, None),
            P("cfg"),
            P(),
            P("hd", None),
            P(("cfg", "th", "tw"), None, "hd"),
            P("hd", None),
            P("hd", None),
            P("hd", ("cfg", "th", "tw")),
        ),
        out_specs=P(None, "th", "tw", ("cfg", "hd")),
        check_vma=False,
    )
```

```python
import functools
import math

import jax
import jax.numpy as jnp
from jax import lax
from jax.experimental import pallas as pl
from jax.experimental.pallas import tpu as pltpu
from jax.sharding import PartitionSpec as P

MESH = pl.DeviceIdType.MESH
BF = jnp.bfloat16
F32 = jnp.float32
VMEM = pl.BlockSpec(memory_space=pltpu.VMEM)
SMEM = pl.BlockSpec(memory_space=pltpu.SMEM)
ANY = pl.BlockSpec(memory_space=pl.ANY)
LIMIT = 62 << 20
TILE = 384
TOK = 1536


def place():
    c, t, w, h = (lax.axis_index(a) for a in ("cfg", "th", "tw", "hd"))
    return c, t, w, h // 4, lax.rem(h, 4)


def partners():
    c, t, w, x, y = place()
    return {
        "left": {"tw": lax.rem(w + 3, 4)},
        "right": {"tw": lax.rem(w + 1, 4)},
        "core": {"th": 1 - t},
        "xl": {"cfg": 1 - c},
        "xh": {"hd": (1 - x) * 4 + y},
        "xd": {"cfg": 1 - c, "hd": (1 - x) * 4 + y},
        "up": {"hd": x * 4 + lax.rem(y + 1, 4)},
        "down": {"hd": x * 4 + lax.rem(y + 3, 4)},
        "yfar": {"hd": x * 4 + lax.rem(y + 2, 4)},
    }


def greet(names):
    to = partners()
    barrier = pltpu.get_barrier_semaphore()
    for name in names:
        pl.semaphore_signal(barrier, inc=1, device_id=to[name], device_id_type=MESH)
    pl.semaphore_wait(barrier, len(names))


class Mail:
    def __init__(self, send, recv):
        self.send, self.recv, self.n, self.all = send, recv, 0, []
        self.to = partners()

    def copy(self, src, dst, name):
        k = self.n
        self.n += 1
        cp = pltpu.make_async_remote_copy(
            src_ref=src,
            dst_ref=dst,
            send_sem=self.send.at[k],
            recv_sem=self.recv.at[k],
            device_id=self.to[name],
            device_id_type=MESH,
        )
        self.all.append(cp)
        return cp

    def post(self, src, dst, name):
        cp = self.copy(src, dst, name)
        cp.start()
        return cp

    def close(self):
        for cp in self.all:
            cp.wait_send()


def normed(v, gain):
    ms = jnp.mean(v * v, axis=-1, keepdims=True)
    return v * lax.rsqrt(ms + 1e-06) * gain


SCALE = math.log2(math.e) / math.sqrt(128.0)


def weights_of(q, keys):
    s = lax.dot_general(q, keys, (((1,), (1,)), ((), ())), preferred_element_type=F32)
    return jnp.exp2(s * SCALE)


GROUP_PIECES = (((1, 0), (2, 0)), ((1, 1), (2, 1)), ((1, 2), (2, 2)), ((0, 0), (0, 1)), ((0, 2),))
N_GROUPS = len(GROUP_PIECES)
BY_Z = (0,)
N_MAIL = 192
EVERYONE = ("left", "right", "core", "xl", "xh", "xd", "up", "down", "yfar")


def sublayer_kernel(
    video, wq, wo, text, qg, kg, off, cnt, guide, out,
    xv, tv, wv0, wv1, wv2, wv3, wv4, woz, woy, wt, qb, tkv, nb0, nb1, nb2, fb0, fb1, fb2, acc_s, den_s,
    att, box, comb, cb, oacc, mid, ends, lsem, ssem, rsem,
):
    c, t, w, x, y = place()
    wv = (wv0, wv1, wv2, wv3, wv4)
    nb = (nb0, nb1, nb2)
    fb = (fb0, fb1, fb2)
    half = 768
    mine = pl.ds(2 * t, 2)
    spot = c * 2 + x
    peers = (("xd", 1 - c, 1 - x), ("xh", c, 1 - x), ("xl", 1 - c, x))

    def rows(cc, tt, ww):
        return pl.ds(pl.multiple_of((cc * 8 + tt * 4 + ww) * 192, 64), 192)

    def half_rows(cc, tt, ww, k):
        return pl.ds(pl.multiple_of((cc * 8 + tt * 4 + ww) * 192 + k * 96, 32), 96)

    own = rows(c, t, w)
    w_loads = []
    n = 4
    for g, pieces in enumerate(GROUP_PIECES):
        for k, (part, h) in enumerate(pieces):
            cp = pltpu.make_async_copy(
                wq.at[part, :, pl.ds(h * 128, 128)], wv[g].at[own, pl.ds(k * 128, 128)], lsem.at[n]
            )
            n += 1
            cp.start()
            w_loads.append(cp)
    for h in range(3):
        cp = pltpu.make_async_copy(wo.at[:, pl.ds(h * 128, 128)], woz.at[w, h], lsem.at[n])
        n += 1
        cp.start()
        w_loads.append(cp)
    loads = [
        pltpu.make_async_copy(video.at[pl.ds(i * half, half)], xv.at[pl.ds(i * half, half)], lsem.at[i])
        for i in range(2)
    ]
    loads.append(pltpu.make_async_copy(text, tv, lsem.at[2]))
    for cp in loads:
        cp.start()
    greet(EVERYONE)
    for cp in w_loads:
        cp.wait()
    mail = Mail(ssem, rsem)
    wl, wr, w2 = lax.rem(w + 3, 4), lax.rem(w + 1, 4), lax.rem(w + 2, 4)
    state = [{} for _ in range(N_GROUPS)]

    def start_own(g, names):
        for name in names:
            state[g][name] = mail.post(wv[g].at[own], wv[g].at[own], name)

    def pass_on(g, key, r, names):
        for tag, name in names:
            state[g][tag] = mail.post(wv[g].at[r], wv[g].at[r], name)

    def z_near(g):
        s = state[g]
        s["right"].wait_recv()
        pass_on(g, "r2", half_rows(c, t, wl, 0), [("r2", "right")])
        pass_on(g, "c1", rows(c, t, wl), [("c1", "core")] + ([] if g in BY_Z else [("x1", "xl")]))
        s["left"].wait_recv()
        pass_on(g, "l2", half_rows(c, t, wr, 1), [("l2", "left")])
        pass_on(g, "c2", rows(c, t, wr), [("c2", "core")] + ([] if g in BY_Z else [("x2", "xl")]))

    def z_far(g):
        s = state[g]
        s["r2"].wait_recv()
        s["l2"].wait_recv()
        pass_on(g, "x3", rows(c, t, w2), [("x3", "xl"), ("c3", "core")])

    def x_near(g):
        state[g]["xl"].wait_recv()
        names = [("d0", "core")]
        if g in BY_Z:
            names = [("x1", "right"), ("x2", "left")] + names
        pass_on(g, "d0", rows(1 - c, t, w), names)

    def x_side(g):
        state[g]["x1"].wait_recv()
        pass_on(g, "d1", rows(1 - c, t, wl), [("d1", "core")])
        state[g]["x2"].wait_recv()
        pass_on(g, "d2", rows(1 - c, t, wr), [("d2", "core")])

    def x_far(g):
        s = state[g]
        s["x3"].wait_recv()
        pass_on(g, "d3", rows(1 - c, t, w2), [("d3", "core")])
        for key in ("core", "c1", "c2", "c3", "d0", "d1", "d2", "d3"):
            s[key].wait_recv()

    def x_events(g):
        x_near(g)
        x_side(g)
        x_far(g)

    def multiply(g):
        ref, pieces = wv[g], GROUP_PIECES[g]

        def step(mc, carry):
            prod = jnp.dot(
                xv[pl.ds(pl.multiple_of(mc * half, half), half), :], ref[...], preferred_element_type=F32
            )
            for k, (part, h) in enumerate(pieces):
                v = prod[:, k * 128 : (k + 1) * 128]
                if part < 2:
                    v = normed(v, (qg if part == 0 else kg)[h : h + 1, :])
                v = v.reshape(3, 2, 8, 2, 8, 128)
                at = pl.ds(pl.multiple_of(mc * 192, 64), 192)
                for i in range(2):
                    for j in range(2):
                        tile = v[:, i, :, j].reshape(192, 128).astype(BF)
                        if part == 0:
                            qb[h, i * 2 + j, at, :] = tile
                        else:
                            nb[h][1 + j, part - 1, 2 * t + i, at, :] = tile
            return carry

        lax.fori_loop(0, 2, step, 0)
        if pieces[0][0] == 1:
            h = pieces[0][1]
            prod = jnp.dot(tv[...], ref[...], preferred_element_type=F32)
            tkv[h, 0] = normed(prod[:, :128], kg[h : h + 1, :]).astype(BF)
            tkv[h, 1] = prod[:, 128:].astype(BF)

    near, far, relays, cores = [None] * 3, [None] * 3, [[], [], []], [None] * 3

    def near_post(h):
        b = nb[h]
        near[h] = (
            (mail.post(b.at[1, :, mine], b.at[3, :, mine], "left"), b.at[3, :, mine]),
            (mail.post(b.at[2, :, mine], b.at[0, :, mine], "right"), b.at[0, :, mine]),
        )
        cores[h] = mail.post(b.at[pl.ds(1, 2), :, mine], b.at[pl.ds(1, 2), :, mine], "core")

    def far_post(h):
        b, f = nb[h], fb[h]
        far[h] = (
            (mail.post(b.at[2, :, mine], f.at[1, :, mine], "left"), f.at[1, :, mine]),
            (mail.post(b.at[1, :, mine], f.at[0, :, mine], "right"), f.at[0, :, mine]),
        )

    def relay(copies):
        passed = []
        for cp, ref in copies:
            cp.wait_recv()
            passed.append(mail.post(ref, ref, "core"))
        return passed

    def await_all(copies):
        for cp in copies:
            cp.wait_recv()

    count = cnt[0]

    def window(h, k):
        i, j = k // 2, lax.rem(k, 2)
        row = jnp.clip(2 * t + i + off[0, h], 1, 2) - 1
        col = jnp.clip(2 * w + j + off[1, h], 1, 6) + 1 - 2 * w
        return row, col, j

    def near_attend(h):
        await_all([cores[h]])

        def tile(k, carry):
            row, col, j = window(h, k)
            q = qb[h, k]
            p = weights_of(q, tkv[h, 0])
            p = jnp.where(lax.broadcasted_iota(jnp.int32, p.shape, 1) < count, p, 0.0)
            den = jnp.sum(p, axis=1, keepdims=True)
            acc = jnp.dot(p.astype(BF), tkv[h, 1], preferred_element_type=F32)
            for d in range(2):
                p = weights_of(q, nb[h][col - j + d, 0, pl.ds(row, 3)].reshape(3 * TILE, 128))
                den = den + jnp.sum(p, axis=1, keepdims=True)
                v = nb[h][col - j + d, 1, pl.ds(row, 3)].reshape(3 * TILE, 128)
                acc = acc + jnp.dot(p.astype(BF), v, preferred_element_type=F32)
            acc_s[h, k] = acc
            den_s[h, k] = jnp.broadcast_to(den, (TILE, 128))
            return carry

        lax.fori_loop(0, 4, tile, 0)

    sends = [None] * 3

    def far_tile(h, k, part=slice(0, TILE)):
        row, col, j = window(h, k)
        last = col + 2 * j
        is_far = jnp.logical_or(last == 0, last == 5)
        at = jnp.clip(last - 1, 0, 3)

        def pick(kind):
            a = fb[h][j, kind, pl.ds(row, 3)].reshape(3 * TILE, 128)
            b = nb[h][at, kind, pl.ds(row, 3)].reshape(3 * TILE, 128)
            return jnp.where(is_far, a, b)

        p = weights_of(qb[h, k, part, :], pick(0))
        den = den_s[h, k, part, :] + jnp.sum(p, axis=1, keepdims=True)
        acc = acc_s[h, k, part, :] + jnp.dot(p.astype(BF), pick(1), preferred_element_type=F32)
        return (acc / den).astype(BF)

    def far_attend(h, pieces=1):
        sends[h] = []
        for a in range(pieces):
            part = slice(a * (TILE // pieces), (a + 1) * (TILE // pieces))
            got = []
            for n, (name, cc, xx) in enumerate(peers):
                att[h, n, part, :] = far_tile(h, cc * 2 + xx, part)
                got.append(mail.post(att.at[h, n, part], box.at[h, spot, part], name))
            box[h, spot, part, :] = far_tile(h, spot, part)
            sends[h].append(got)

    y_got = [None] * 3
    gs = guide[0]
    y_lane = pl.ds(pl.multiple_of(y * 128, 128), 128)

    def mix(h, a=0, pieces=1):
        part = slice(a * (TILE // pieces), (a + 1) * (TILE // pieces))
        await_all(sends[h][a])
        for xx in range(2):
            mixed = gs * box[h, xx, part, :].astype(F32) + (1.0 - gs) * box[h, 2 + xx, part, :].astype(F32)
            comb[h, xx, part, :] = mixed.astype(BF)
        src = comb.at[h, :, part]
        y_got[h] = [mail.post(src, cb.at[h, :, part, y_lane], name) for name in ("yfar", "up", "down")]
        for xx in range(2):
            cb[h, xx, part, y_lane] = comb[h, xx, part, :]
        return y_got[h]

    def term(h, cc, xx, part=slice(0, TILE)):
        total = None
        for k in range(2):
            prod = lax.dot_general(
                cb[h, k, part, :], wt[h, k, cc, xx], (((1,), (1,)), ((), ())), preferred_element_type=F32
            )
            total = prod if total is None else total + prod
        return total

    def early_product(h):
        await_all(y_got[h])

        def dest(d, carry):
            cc, xx = d // 2, lax.rem(d, 2)
            if h == 0:
                oacc[d] = term(h, cc, xx)
            else:
                oacc[d] += term(h, cc, xx)
            return carry

        lax.fori_loop(0, 4, dest, 0)

    start_own(0, ("left", "right", "xl", "core"))
    start_own(1, ("left", "right", "xl", "core"))
    o_left = mail.post(woz.at[w], woz.at[w], "left")
    o_right = mail.post(woz.at[w], woz.at[w], "right")
    z_near(0)
    x_near(0)
    start_own(2, ("left", "right", "core"))
    z_far(0)
    z_near(1)
    x_side(0)
    start_own(2, ("xl",))
    start_own(3, ("left", "right", "core"))
    start_own(4, ("left", "right", "core"))
    z_far(1)
    o_right.wait_recv()
    o_r2 = mail.post(woz.at[wl, :, pl.ds(0, 96)], woz.at[wl, :, pl.ds(0, 96)], "right")
    o_left.wait_recv()
    o_l2 = mail.post(woz.at[wr, :, pl.ds(96, 96)], woz.at[wr, :, pl.ds(96, 96)], "left")
    z_near(2)
    z_far(2)
    start_own(3, ("xl",))
    start_own(4, ("xl",))
    x_far(0)
    for cp in loads:
        cp.wait()
    multiply(0)
    near_post(0)
    z_near(3)
    z_near(4)
    o_r2.wait_recv()
    o_l2.wait_recv()
    o_y = []
    for name, yy in (("up", lax.rem(y + 1, 4)), ("down", lax.rem(y + 3, 4)), ("yfar", lax.rem(y + 2, 4))):
        o_y.append(mail.post(woz.at[yy], woy.at[:, :, y_lane], name))
    woy[:, :, y_lane] = woz[y]
    x_events(1)
    multiply(1)
    near_post(1)
    far_post(0)
    x_events(2)
    multiply(2)
    near_post(2)
    far_post(1)
    far_post(2)
    z_far(3)
    z_far(4)
    await_all(o_y)
    o_xl = mail.post(woy, wt.at[:, x, c, t], "xl")
    o_xd = mail.post(woy, wt.at[:, x, c, t], "xd")
    o_core = [mail.post(woy, wt.at[:, x, c, t], "core")]
    o_keep = pltpu.make_async_copy(woy, wt.at[:, x, c, t], lsem.at[3])
    o_keep.start()
    relays[0] += relay(near[0])
    x_events(3)
    multiply(3)
    await_all(relays[0])
    near_attend(0)
    relays[1] += relay(near[1])
    x_events(4)
    multiply(4)
    await_all(relays[1])
    near_attend(1)
    tail = relay(far[0])
    relays[2] += relay(near[2])
    o_xl.wait_recv()
    at = wt.at[:, x, 1 - c, t]
    o_core.append(mail.post(at, at, "core"))
    o_xf = mail.post(at, at, "xd")
    o_xd.wait_recv()
    at = wt.at[:, 1 - x, 1 - c, t]
    o_core.append(mail.post(at, at, "core"))
    await_all(tail)
    far_attend(0)
    await_all(relays[2])
    near_attend(2)
    mix(0)
    tail = relay(far[1])
    await_all(tail)
    far_attend(1)
    o_xf.wait_recv()
    at = wt.at[:, 1 - x, c, t]
    o_core.append(mail.post(at, at, "core"))
    mix(1)
    o_keep.wait()
    await_all(o_core)
    early_product(0)
    tail = relay(far[2])
    await_all(tail)
    far_attend(2, 2)
    early_product(1)
    y_half = [mix(2, 0, 2), mix(2, 1, 2)]
    last = []
    for a in range(2):
        part = slice(a * 192, (a + 1) * 192)
        await_all(y_half[a])
        for n, (name, cc, xx) in enumerate(peers):
            mid[n, part, :] = (oacc[cc * 2 + xx, part, :] + term(2, cc, xx, part)).astype(BF)
            last.append(mail.post(mid.at[n, part], ends.at[spot, part], name))
        ends[spot, part, :] = (oacc[spot, part, :] + term(2, c, x, part)).astype(BF)
    await_all(last)
    for i in range(2):
        sides = [ends[i * 2 + j].astype(F32).reshape(6, 8, 8, 192) for j in range(2)]
        out[:, i * 8 : (i + 1) * 8] = jnp.concatenate(sides, axis=2).astype(BF)
    mail.close()


def sublayer(video, wq, wo, text, qg, kg, off, cnt, guide):
    near = pltpu.VMEM((4, 2, 4, TILE, 128), BF)
    far = pltpu.VMEM((2, 2, 4, TILE, 128), BF)
    return pl.pallas_call(
        sublayer_kernel,
        out_shape=jax.ShapeDtypeStruct((6, 16, 16, 192), BF),
        in_specs=[ANY, ANY, ANY, ANY, VMEM, VMEM, SMEM, SMEM, SMEM],
        out_specs=VMEM,
        scratch_shapes=[
            pltpu.VMEM((TOK, 3072), BF),
            pltpu.VMEM((256, 3072), BF),
            pltpu.VMEM((3072, 256), BF),
            pltpu.VMEM((3072, 256), BF),
            pltpu.VMEM((3072, 256), BF),
            pltpu.VMEM((3072, 256), BF),
            pltpu.VMEM((3072, 128), BF),
            pltpu.VMEM((4, 3, 192, 128), BF),
            pltpu.VMEM((3, 192, 512), BF),
            pltpu.VMEM((3, 2, 2, 2, 192, 512), BF),
            pltpu.VMEM((3, 4, TILE, 128), BF),
            pltpu.VMEM((3, 2, 256, 128), BF),
            near,
            near,
            near,
            far,
            far,
            far,
            pltpu.VMEM((3, 4, TILE, 128), F32),
            pltpu.VMEM((3, 4, TILE, 128), F32),
            pltpu.VMEM((3, 3, TILE, 128), BF),
            pltpu.VMEM((3, 4, TILE, 128), BF),
            pltpu.VMEM((3, 2, TILE, 128), BF),
            pltpu.VMEM((3, 2, TILE, 512), BF),
            pltpu.VMEM((4, TILE, 192), F32),
            pltpu.VMEM((3, TILE, 192), BF),
            pltpu.VMEM((4, TILE, 192), BF),
            pltpu.SemaphoreType.DMA((20,)),
            pltpu.SemaphoreType.DMA((N_MAIL,)),
            pltpu.SemaphoreType.DMA((N_MAIL,)),
        ],
        compiler_params=pltpu.CompilerParams(collective_id=0, has_side_effects=True, vmem_limit_bytes=LIMIT),
    )(video, wq, wo, text, qg, kg, off, cnt, guide)


def body(video, text_states, text_count, guidance, window_offsets, w_qkv, q_gain, k_gain, w_out):
    return sublayer(
        video.reshape(TOK, 3072),
        w_qkv.swapaxes(0, 1),
        w_out.T,
        text_states[0],
        q_gain,
        k_gain,
        window_offsets.T,
        text_count,
        guidance,
    )


def solution(mesh):
    return jax.shard_map(
        body,
        mesh=mesh,
        in_specs=(
            P("cfg", None, "th", "tw", None),
            P("cfg", None, None),
            P("cfg"),
            P(),
            P("hd", None),
            P(("cfg", "th", "tw"), None, "hd"),
            P("hd", None),
            P("hd", None),
            P("hd", ("cfg", "th", "tw")),
        ),
        out_specs=P(None, "th", "tw", ("cfg", "hd")),
        check_vma=False,
    )
```

```python
import functools
import math

import jax
import jax.numpy as jnp
from jax import lax
from jax.experimental import pallas as pl
from jax.experimental.pallas import tpu as pltpu
from jax.sharding import PartitionSpec as P

MESH = pl.DeviceIdType.MESH
BF = jnp.bfloat16
F32 = jnp.float32
VMEM = pl.BlockSpec(memory_space=pltpu.VMEM)
SMEM = pl.BlockSpec(memory_space=pltpu.SMEM)
ANY = pl.BlockSpec(memory_space=pl.ANY)
LIMIT = 62 << 20
TILE = 384
TOK = 1536


def place():
    c, t, w, h = (lax.axis_index(a) for a in ("cfg", "th", "tw", "hd"))
    return c, t, w, h // 4, lax.rem(h, 4)


def partners():
    c, t, w, x, y = place()
    return {
        "left": {"tw": lax.rem(w + 3, 4)},
        "right": {"tw": lax.rem(w + 1, 4)},
        "core": {"th": 1 - t},
        "xl": {"cfg": 1 - c},
        "xh": {"hd": (1 - x) * 4 + y},
        "xd": {"cfg": 1 - c, "hd": (1 - x) * 4 + y},
        "up": {"hd": x * 4 + lax.rem(y + 1, 4)},
        "down": {"hd": x * 4 + lax.rem(y + 3, 4)},
        "yfar": {"hd": x * 4 + lax.rem(y + 2, 4)},
    }


def greet(names):
    to = partners()
    barrier = pltpu.get_barrier_semaphore()
    for name in names:
        pl.semaphore_signal(barrier, inc=1, device_id=to[name], device_id_type=MESH)
    pl.semaphore_wait(barrier, len(names))


class Mail:
    def __init__(self, send, recv):
        self.send, self.recv, self.n, self.all = send, recv, 0, []
        self.to = partners()

    def copy(self, src, dst, name):
        k = self.n
        self.n += 1
        cp = pltpu.make_async_remote_copy(
            src_ref=src,
            dst_ref=dst,
            send_sem=self.send.at[k],
            recv_sem=self.recv.at[k],
            device_id=self.to[name],
            device_id_type=MESH,
        )
        self.all.append(cp)
        return cp

    def post(self, src, dst, name):
        cp = self.copy(src, dst, name)
        cp.start()
        return cp

    def close(self):
        for cp in self.all:
            cp.wait_send()


def normed(v, gain):
    ms = jnp.mean(v * v, axis=-1, keepdims=True)
    return v * lax.rsqrt(ms + 1e-06) * gain


SCALE = math.log2(math.e) / math.sqrt(128.0)


def weights_of(q, keys):
    s = lax.dot_general(q, keys, (((1,), (1,)), ((), ())), preferred_element_type=F32)
    return jnp.exp2(s * SCALE)


GROUP_PIECES = (((1, 0), (2, 0)), ((0, 0), (0, 1)), ((1, 1), (2, 1)), ((1, 2), (2, 2)), ((0, 2),))
N_GROUPS = len(GROUP_PIECES)
BY_Z = (0,)
FRAMES = 3
PIECES = 2
N_MAIL = 224
EVERYONE = ("left", "right", "core", "xl", "xh", "xd", "up", "down", "yfar")


def sublayer_kernel(
    video, wq, wo, text, qg, kg, off, cnt, guide, out,
    xv, tv, wv0, wv1, wv2, wv3, wv4, woz, woy, wt, qb, tkv, nb0, nb1, nb2, fb0, fb1, fb2, acc_s, den_s,
    att, box, comb, cb, oacc, mid, ends, lsem, ssem, rsem,
):
    c, t, w, x, y = place()
    wv = (wv0, wv1, wv2, wv3, wv4)
    nb = (nb0, nb1, nb2)
    fb = (fb0, fb1, fb2)
    half = 768
    mine = pl.ds(2 * t, 2)
    spot = c * 2 + x
    peers = (("xd", 1 - c, 1 - x), ("xh", c, 1 - x), ("xl", 1 - c, x))

    def rows(cc, tt, ww):
        return pl.ds(pl.multiple_of((cc * 8 + tt * 4 + ww) * 192, 64), 192)

    def half_rows(cc, tt, ww, k):
        return pl.ds(pl.multiple_of((cc * 8 + tt * 4 + ww) * 192 + k * 96, 32), 96)

    own = rows(c, t, w)
    w_loads = []
    n = 4
    for g, pieces in enumerate(GROUP_PIECES):
        for k, (part, h) in enumerate(pieces):
            cp = pltpu.make_async_copy(
                wq.at[part, :, pl.ds(h * 128, 128)], wv[g].at[own, pl.ds(k * 128, 128)], lsem.at[n]
            )
            n += 1
            cp.start()
            w_loads.append(cp)
    for h in range(3):
        cp = pltpu.make_async_copy(wo.at[:, pl.ds(h * 128, 128)], woz.at[w, h], lsem.at[n])
        n += 1
        cp.start()
        w_loads.append(cp)
    loads = [
        pltpu.make_async_copy(video.at[pl.ds(i * half, half)], xv.at[pl.ds(i * half, half)], lsem.at[i])
        for i in range(2)
    ]
    loads.append(pltpu.make_async_copy(text, tv, lsem.at[2]))
    for cp in loads:
        cp.start()
    greet(EVERYONE)
    for cp in w_loads:
        cp.wait()
    mail = Mail(ssem, rsem)
    wl, wr, w2 = lax.rem(w + 3, 4), lax.rem(w + 1, 4), lax.rem(w + 2, 4)
    state = [{} for _ in range(N_GROUPS)]

    def start_own(g, names):
        for name in names:
            state[g][name] = mail.post(wv[g].at[own], wv[g].at[own], name)

    def pass_on(g, key, r, names):
        for tag, name in names:
            state[g][tag] = mail.post(wv[g].at[r], wv[g].at[r], name)

    def z_near(g):
        s = state[g]
        s["right"].wait_recv()
        pass_on(g, "r2", half_rows(c, t, wl, 0), [("r2", "right")])
        pass_on(g, "c1", rows(c, t, wl), [("c1", "core")] + ([] if g in BY_Z else [("x1", "xl")]))
        s["left"].wait_recv()
        pass_on(g, "l2", half_rows(c, t, wr, 1), [("l2", "left")])
        pass_on(g, "c2", rows(c, t, wr), [("c2", "core")] + ([] if g in BY_Z else [("x2", "xl")]))

    def z_far(g):
        s = state[g]
        s["r2"].wait_recv()
        s["l2"].wait_recv()
        pass_on(g, "x3", rows(c, t, w2), [("x3", "xl"), ("c3", "core")])

    def x_near(g):
        state[g]["xl"].wait_recv()
        names = [("d0", "core")]
        if g in BY_Z:
            names = [("x1", "right"), ("x2", "left")] + names
        pass_on(g, "d0", rows(1 - c, t, w), names)

    def x_side(g):
        state[g]["x1"].wait_recv()
        pass_on(g, "d1", rows(1 - c, t, wl), [("d1", "core")])
        state[g]["x2"].wait_recv()
        pass_on(g, "d2", rows(1 - c, t, wr), [("d2", "core")])

    def x_far(g):
        s = state[g]
        s["x3"].wait_recv()
        pass_on(g, "d3", rows(1 - c, t, w2), [("d3", "core")])
        for key in ("core", "c1", "c2", "c3", "d0", "d1", "d2", "d3"):
            s[key].wait_recv()

    def x_events(g):
        x_near(g)
        x_side(g)
        x_far(g)

    def multiply(g):
        ref, pieces = wv[g], GROUP_PIECES[g]

        frames = FRAMES
        half = 256 * frames

        def step(mc, carry):
            prod = jnp.dot(
                xv[pl.ds(pl.multiple_of(mc * half, half), half), :], ref[...], preferred_element_type=F32
            )
            for k, (part, h) in enumerate(pieces):
                v = prod[:, k * 128 : (k + 1) * 128]
                if part < 2:
                    v = normed(v, (qg if part == 0 else kg)[h : h + 1, :])
                v = v.reshape(frames, 2, 8, 2, 8, 128)
                at = pl.ds(pl.multiple_of(mc * 64 * frames, 64), 64 * frames)
                for i in range(2):
                    for j in range(2):
                        tile = v[:, i, :, j].reshape(64 * frames, 128).astype(BF)
                        if part == 0:
                            qb[h, i * 2 + j, at, :] = tile
                        else:
                            nb[h][1 + j, part - 1, 2 * t + i, at, :] = tile
            return carry

        lax.fori_loop(0, 6 // frames, step, 0)
        if pieces[0][0] == 1:
            h = pieces[0][1]
            prod = jnp.dot(tv[...], ref[...], preferred_element_type=F32)
            tkv[h, 0] = normed(prod[:, :128], kg[h : h + 1, :]).astype(BF)
            tkv[h, 1] = prod[:, 128:].astype(BF)

    near, far, relays, cores = [None] * 3, [None] * 3, [[], [], []], [None] * 3

    def near_post(h):
        b = nb[h]
        near[h] = (
            (mail.post(b.at[1, :, mine], b.at[3, :, mine], "left"), b.at[3, :, mine]),
            (mail.post(b.at[2, :, mine], b.at[0, :, mine], "right"), b.at[0, :, mine]),
        )
        cores[h] = mail.post(b.at[pl.ds(1, 2), :, mine], b.at[pl.ds(1, 2), :, mine], "core")

    def far_post(h):
        b, f = nb[h], fb[h]
        far[h] = (
            (mail.post(b.at[2, :, mine], f.at[1, :, mine], "left"), f.at[1, :, mine]),
            (mail.post(b.at[1, :, mine], f.at[0, :, mine], "right"), f.at[0, :, mine]),
        )

    def relay(copies):
        passed = []
        for cp, ref in copies:
            cp.wait_recv()
            passed.append(mail.post(ref, ref, "core"))
        return passed

    def await_all(copies):
        for cp in copies:
            cp.wait_recv()

    count = cnt[0]

    def window(h, k):
        i, j = k // 2, lax.rem(k, 2)
        row = jnp.clip(2 * t + i + off[0, h], 1, 2) - 1
        col = jnp.clip(2 * w + j + off[1, h], 1, 6) + 1 - 2 * w
        return row, col, j

    def near_attend(h):
        await_all([cores[h]])

        def tile(k, carry):
            row, col, j = window(h, k)
            q = qb[h, k]
            p = weights_of(q, tkv[h, 0])
            p = jnp.where(lax.broadcasted_iota(jnp.int32, p.shape, 1) < count, p, 0.0)
            den = jnp.sum(p, axis=1, keepdims=True)
            acc = jnp.dot(p.astype(BF), tkv[h, 1], preferred_element_type=F32)
            for d in range(2):
                p = weights_of(q, nb[h][col - j + d, 0, pl.ds(row, 3)].reshape(3 * TILE, 128))
                den = den + jnp.sum(p, axis=1, keepdims=True)
                v = nb[h][col - j + d, 1, pl.ds(row, 3)].reshape(3 * TILE, 128)
                acc = acc + jnp.dot(p.astype(BF), v, preferred_element_type=F32)
            acc_s[h, k] = acc
            den_s[h, k] = jnp.broadcast_to(den, (TILE, 128))
            return carry

        lax.fori_loop(0, 4, tile, 0)

    sends = [None] * 3

    def far_tile(h, k, part=slice(0, TILE)):
        row, col, j = window(h, k)
        last = col + 2 * j
        is_far = jnp.logical_or(last == 0, last == 5)
        at = jnp.clip(last - 1, 0, 3)

        def pick(kind):
            a = fb[h][j, kind, pl.ds(row, 3)].reshape(3 * TILE, 128)
            b = nb[h][at, kind, pl.ds(row, 3)].reshape(3 * TILE, 128)
            return jnp.where(is_far, a, b)

        p = weights_of(qb[h, k, part, :], pick(0))
        den = den_s[h, k, part, :] + jnp.sum(p, axis=1, keepdims=True)
        acc = acc_s[h, k, part, :] + jnp.dot(p.astype(BF), pick(1), preferred_element_type=F32)
        return (acc / den).astype(BF)

    def far_attend(h):
        def tile(k, carry):
            att[h, k] = far_tile(h, k)
            return carry

        lax.fori_loop(0, 4, tile, 0)
        sends[h] = [mail.post(att.at[h, cc * 2 + xx], box.at[h, spot], name) for name, cc, xx in peers]
        box[h, spot] = att[h, spot]

    y_got = [None] * 3
    gs = guide[0]
    y_lane = pl.ds(pl.multiple_of(y * 128, 128), 128)

    def mix(h, a=0, pieces=1):
        part = slice(a * (TILE // pieces), (a + 1) * (TILE // pieces))
        if a == 0:
            await_all(sends[h])
        for xx in range(2):
            mixed = gs * box[h, xx, part, :].astype(F32) + (1.0 - gs) * box[h, 2 + xx, part, :].astype(F32)
            comb[h, xx, part, :] = mixed.astype(BF)
        src = comb.at[h, :, part]
        y_got[h] = [mail.post(src, cb.at[h, :, part, y_lane], name) for name in ("yfar", "up", "down")]
        for xx in range(2):
            cb[h, xx, part, y_lane] = comb[h, xx, part, :]
        return y_got[h]

    def term(h, cc, xx, part=slice(0, TILE)):
        total = None
        for k in range(2):
            prod = lax.dot_general(
                cb[h, k, part, :], wt[h, k, cc, xx], (((1,), (1,)), ((), ())), preferred_element_type=F32
            )
            total = prod if total is None else total + prod
        return total

    def early_product(h):
        await_all(y_got[h])

        def dest(d, carry):
            cc, xx = d // 2, lax.rem(d, 2)
            if h == 0:
                oacc[d] = term(h, cc, xx)
            else:
                oacc[d] += term(h, cc, xx)
            return carry

        lax.fori_loop(0, 4, dest, 0)

    start_own(0, ("left", "right", "xl", "core"))
    start_own(1, ("left", "right", "xl", "core"))
    o_left = mail.post(woz.at[w], woz.at[w], "left")
    o_right = mail.post(woz.at[w], woz.at[w], "right")
    z_near(0)
    x_near(0)
    start_own(2, ("left", "right", "core", "xl"))
    z_far(0)
    z_near(1)
    x_side(0)
    start_own(3, ("left", "right", "core"))
    start_own(4, ("left", "right", "core"))
    z_far(1)
    o_right.wait_recv()
    o_r2 = mail.post(woz.at[wl, :, pl.ds(0, 96)], woz.at[wl, :, pl.ds(0, 96)], "right")
    o_left.wait_recv()
    o_l2 = mail.post(woz.at[wr, :, pl.ds(96, 96)], woz.at[wr, :, pl.ds(96, 96)], "left")
    z_near(2)
    z_far(2)
    start_own(3, ("xl",))
    x_far(0)
    z_near(3)
    start_own(4, ("xl",))
    z_near(4)
    for cp in loads:
        cp.wait()
    multiply(0)
    near_post(0)
    far_post(0)
    z_far(3)
    z_far(4)
    o_r2.wait_recv()
    o_l2.wait_recv()
    o_y = []
    for name, yy in (("up", lax.rem(y + 1, 4)), ("down", lax.rem(y + 3, 4)), ("yfar", lax.rem(y + 2, 4))):
        o_y.append(mail.post(woz.at[yy], woy.at[:, :, y_lane], name))
    woy[:, :, y_lane] = woz[y]
    x_events(1)
    multiply(1)
    x_events(2)
    multiply(2)
    near_post(1)
    far_post(1)
    await_all(o_y)
    o_xl, o_xd, o_xf, o_core = [None] * 3, [None] * 3, [None] * 3, [[], [], []]
    for h in range(3):
        o_xl[h] = mail.post(woy.at[h], wt.at[h, x, c, t], "xl")
        o_xd[h] = mail.post(woy.at[h], wt.at[h, x, c, t], "xd")
        o_core[h].append(mail.post(woy.at[h], wt.at[h, x, c, t], "core"))

    def o_cross(h):
        o_xl[h].wait_recv()
        at = wt.at[h, x, 1 - c, t]
        o_core[h].append(mail.post(at, at, "core"))
        o_xf[h] = mail.post(at, at, "xd")
        o_xd[h].wait_recv()
        at = wt.at[h, 1 - x, 1 - c, t]
        o_core[h].append(mail.post(at, at, "core"))

    def o_last(h):
        o_xf[h].wait_recv()
        at = wt.at[h, 1 - x, c, t]
        o_core[h].append(mail.post(at, at, "core"))

    o_keep = pltpu.make_async_copy(woy, wt.at[:, x, c, t], lsem.at[3])
    o_keep.start()
    relays[0] += relay(near[0])
    await_all(relays[0])
    near_attend(0)
    x_events(3)
    multiply(3)
    near_post(2)
    far_post(2)
    tail = relay(far[0])
    await_all(tail)
    far_attend(0)
    x_events(4)
    multiply(4)
    relays[1] += relay(near[1])
    await_all(relays[1])
    o_cross(0)
    near_attend(1)
    tail = relay(far[1])
    mix(0)
    o_cross(1)
    await_all(tail)
    far_attend(1)
    o_cross(2)
    relays[2] += relay(near[2])
    await_all(relays[2])
    near_attend(2)
    mix(1)
    tail = relay(far[2])
    await_all(tail)
    far_attend(2)
    o_keep.wait()
    for h in range(3):
        o_last(h)
    await_all(o_core[0])
    early_product(0)
    await_all(o_core[1])
    early_product(1)
    await_all(o_core[2])
    y_parts = [mix(2, a, PIECES) for a in range(PIECES)]
    last = []
    for a in range(PIECES):
        part = slice(a * (TILE // PIECES), (a + 1) * (TILE // PIECES))
        await_all(y_parts[a])
        for n, (name, cc, xx) in enumerate(peers):
            mid[n, part, :] = (oacc[cc * 2 + xx, part, :] + term(2, cc, xx, part)).astype(BF)
            last.append(mail.post(mid.at[n, part], ends.at[spot, part], name))
        ends[spot, part, :] = (oacc[spot, part, :] + term(2, c, x, part)).astype(BF)
    await_all(last)
    for i in range(2):
        sides = [ends[i * 2 + j].astype(F32).reshape(6, 8, 8, 192) for j in range(2)]
        out[:, i * 8 : (i + 1) * 8] = jnp.concatenate(sides, axis=2).astype(BF)
    mail.close()


def sublayer(video, wq, wo, text, qg, kg, off, cnt, guide):
    near = pltpu.VMEM((4, 2, 4, TILE, 128), BF)
    far = pltpu.VMEM((2, 2, 4, TILE, 128), BF)
    return pl.pallas_call(
        sublayer_kernel,
        out_shape=jax.ShapeDtypeStruct((6, 16, 16, 192), BF),
        in_specs=[ANY, ANY, ANY, ANY, VMEM, VMEM, SMEM, SMEM, SMEM],
        out_specs=VMEM,
        scratch_shapes=[
            pltpu.VMEM((TOK, 3072), BF),
            pltpu.VMEM((256, 3072), BF),
            pltpu.VMEM((3072, 256), BF),
            pltpu.VMEM((3072, 256), BF),
            pltpu.VMEM((3072, 256), BF),
            pltpu.VMEM((3072, 256), BF),
            pltpu.VMEM((3072, 128), BF),
            pltpu.VMEM((4, 3, 192, 128), BF),
            pltpu.VMEM((3, 192, 512), BF),
            pltpu.VMEM((3, 2, 2, 2, 192, 512), BF),
            pltpu.VMEM((3, 4, TILE, 128), BF),
            pltpu.VMEM((3, 2, 256, 128), BF),
            near,
            near,
            near,
            far,
            far,
            far,
            pltpu.VMEM((3, 4, TILE, 128), F32),
            pltpu.VMEM((3, 4, TILE, 128), F32),
            pltpu.VMEM((3, 4, TILE, 128), BF),
            pltpu.VMEM((3, 4, TILE, 128), BF),
            pltpu.VMEM((3, 2, TILE, 128), BF),
            pltpu.VMEM((3, 2, TILE, 512), BF),
            pltpu.VMEM((4, TILE, 192), F32),
            pltpu.VMEM((3, TILE, 192), BF),
            pltpu.VMEM((4, TILE, 192), BF),
            pltpu.SemaphoreType.DMA((20,)),
            pltpu.SemaphoreType.DMA((N_MAIL,)),
            pltpu.SemaphoreType.DMA((N_MAIL,)),
        ],
        compiler_params=pltpu.CompilerParams(collective_id=0, has_side_effects=True, vmem_limit_bytes=LIMIT),
    )(video, wq, wo, text, qg, kg, off, cnt, guide)


def body(video, text_states, text_count, guidance, window_offsets, w_qkv, q_gain, k_gain, w_out):
    return sublayer(
        video.reshape(TOK, 3072),
        w_qkv.swapaxes(0, 1),
        w_out.T,
        text_states[0],
        q_gain,
        k_gain,
        window_offsets.T,
        text_count,
        guidance,
    )


def solution(mesh):
    return jax.shard_map(
        body,
        mesh=mesh,
        in_specs=(
            P("cfg", None, "th", "tw", None),
            P("cfg", None, None),
            P("cfg"),
            P(),
            P("hd", None),
            P(("cfg", "th", "tw"), None, "hd"),
            P("hd", None),
            P("hd", None),
            P("hd", ("cfg", "th", "tw")),
        ),
        out_specs=P(None, "th", "tw", ("cfg", "hd")),
        check_vma=False,
    )
```

```python
import functools
import math

import jax
import jax.numpy as jnp
from jax import lax
from jax.experimental import pallas as pl
from jax.experimental.pallas import tpu as pltpu
from jax.sharding import PartitionSpec as P

MESH = pl.DeviceIdType.MESH
BF = jnp.bfloat16
F32 = jnp.float32
VMEM = pl.BlockSpec(memory_space=pltpu.VMEM)
SMEM = pl.BlockSpec(memory_space=pltpu.SMEM)
ANY = pl.BlockSpec(memory_space=pl.ANY)
LIMIT = 62 << 20
TILE = 384
TOK = 1536


def place():
    c, t, w, h = (lax.axis_index(a) for a in ("cfg", "th", "tw", "hd"))
    return c, t, w, h // 4, lax.rem(h, 4)


def partners():
    c, t, w, x, y = place()
    return {
        "left": {"tw": lax.rem(w + 3, 4)},
        "right": {"tw": lax.rem(w + 1, 4)},
        "core": {"th": 1 - t},
        "xl": {"cfg": 1 - c},
        "xh": {"hd": (1 - x) * 4 + y},
        "xd": {"cfg": 1 - c, "hd": (1 - x) * 4 + y},
        "up": {"hd": x * 4 + lax.rem(y + 1, 4)},
        "down": {"hd": x * 4 + lax.rem(y + 3, 4)},
        "yfar": {"hd": x * 4 + lax.rem(y + 2, 4)},
    }


def greet(names):
    to = partners()
    barrier = pltpu.get_barrier_semaphore()
    for name in names:
        pl.semaphore_signal(barrier, inc=1, device_id=to[name], device_id_type=MESH)
    pl.semaphore_wait(barrier, len(names))


class Mail:
    def __init__(self, send, recv):
        self.send, self.recv, self.n, self.all = send, recv, 0, []
        self.to = partners()

    def copy(self, src, dst, name):
        k = self.n
        self.n += 1
        cp = pltpu.make_async_remote_copy(
            src_ref=src,
            dst_ref=dst,
            send_sem=self.send.at[k],
            recv_sem=self.recv.at[k],
            device_id=self.to[name],
            device_id_type=MESH,
        )
        self.all.append(cp)
        return cp

    def post(self, src, dst, name):
        cp = self.copy(src, dst, name)
        cp.start()
        return cp

    def close(self):
        for cp in self.all:
            cp.wait_send()


def normed(v, gain):
    ms = jnp.mean(v * v, axis=-1, keepdims=True)
    return v * lax.rsqrt(ms + 1e-06) * gain


SCALE = math.log2(math.e) / math.sqrt(128.0)


def weights_of(q, keys):
    s = lax.dot_general(q, keys, (((1,), (1,)), ((), ())), preferred_element_type=F32)
    return jnp.exp2(s * SCALE)


GROUP_PIECES = (((1, 0), (2, 0)), ((1, 1), (2, 1)), ((0, 0), (0, 1)), ((1, 2), (2, 2)), ((0, 2),))
N_GROUPS = len(GROUP_PIECES)
BY_Z = (0,)
FRAMES = 3
PIECES = 4
N_MAIL = 224
EVERYONE = ("left", "right", "core", "xl", "xh", "xd", "up", "down", "yfar")


def sublayer_kernel(
    video, wq, wo, text, qg, kg, off, cnt, guide, out,
    xv, tv, wv0, wv1, wv2, wv3, wv4, woz, woy, wt, qb, tkv, nb0, nb1, nb2, fb0, fb1, fb2, acc_s, den_s,
    att, box, comb, cb, oacc, mid, ends, lsem, ssem, rsem,
):
    c, t, w, x, y = place()
    wv = (wv0, wv1, wv2, wv3, wv4)
    nb = (nb0, nb1, nb2)
    fb = (fb0, fb1, fb2)
    half = 768
    mine = pl.ds(2 * t, 2)
    spot = c * 2 + x
    peers = (("xd", 1 - c, 1 - x), ("xh", c, 1 - x), ("xl", 1 - c, x))

    def rows(cc, tt, ww):
        return pl.ds(pl.multiple_of((cc * 8 + tt * 4 + ww) * 192, 64), 192)

    def half_rows(cc, tt, ww, k):
        return pl.ds(pl.multiple_of((cc * 8 + tt * 4 + ww) * 192 + k * 96, 32), 96)

    own = rows(c, t, w)
    w_loads = []
    n = 4
    for g, pieces in enumerate(GROUP_PIECES):
        for k, (part, h) in enumerate(pieces):
            cp = pltpu.make_async_copy(
                wq.at[part, :, pl.ds(h * 128, 128)], wv[g].at[own, pl.ds(k * 128, 128)], lsem.at[n]
            )
            n += 1
            cp.start()
            w_loads.append(cp)
    for h in range(3):
        cp = pltpu.make_async_copy(wo.at[:, pl.ds(h * 128, 128)], woz.at[w, h], lsem.at[n])
        n += 1
        cp.start()
        w_loads.append(cp)
    loads = [
        pltpu.make_async_copy(video.at[pl.ds(i * half, half)], xv.at[pl.ds(i * half, half)], lsem.at[i])
        for i in range(2)
    ]
    loads.append(pltpu.make_async_copy(text, tv, lsem.at[2]))
    for cp in loads:
        cp.start()
    greet(EVERYONE)
    for cp in w_loads:
        cp.wait()
    mail = Mail(ssem, rsem)
    wl, wr, w2 = lax.rem(w + 3, 4), lax.rem(w + 1, 4), lax.rem(w + 2, 4)
    state = [{} for _ in range(N_GROUPS)]

    def start_own(g, names):
        for name in names:
            state[g][name] = mail.post(wv[g].at[own], wv[g].at[own], name)

    def pass_on(g, key, r, names):
        for tag, name in names:
            state[g][tag] = mail.post(wv[g].at[r], wv[g].at[r], name)

    def z_near(g):
        s = state[g]
        s["right"].wait_recv()
        pass_on(g, "r2", half_rows(c, t, wl, 0), [("r2", "right")])
        pass_on(g, "c1", rows(c, t, wl), [("c1", "core")] + ([] if g in BY_Z else [("x1", "xl")]))
        s["left"].wait_recv()
        pass_on(g, "l2", half_rows(c, t, wr, 1), [("l2", "left")])
        pass_on(g, "c2", rows(c, t, wr), [("c2", "core")] + ([] if g in BY_Z else [("x2", "xl")]))

    def z_far(g):
        s = state[g]
        s["r2"].wait_recv()
        s["l2"].wait_recv()
        pass_on(g, "x3", rows(c, t, w2), [("x3", "xl"), ("c3", "core")])

    def x_near(g):
        state[g]["xl"].wait_recv()
        names = [("d0", "core")]
        if g in BY_Z:
            names = [("x1", "right"), ("x2", "left")] + names
        pass_on(g, "d0", rows(1 - c, t, w), names)

    def x_side(g):
        state[g]["x1"].wait_recv()
        pass_on(g, "d1", rows(1 - c, t, wl), [("d1", "core")])
        state[g]["x2"].wait_recv()
        pass_on(g, "d2", rows(1 - c, t, wr), [("d2", "core")])

    def x_far(g):
        s = state[g]
        s["x3"].wait_recv()
        pass_on(g, "d3", rows(1 - c, t, w2), [("d3", "core")])
        for key in ("core", "c1", "c2", "c3", "d0", "d1", "d2", "d3"):
            s[key].wait_recv()

    def x_events(g):
        x_near(g)
        x_side(g)
        x_far(g)

    def multiply(g):
        ref, pieces = wv[g], GROUP_PIECES[g]

        frames = FRAMES
        half = 256 * frames

        def step(mc, carry):
            prod = jnp.dot(
                xv[pl.ds(pl.multiple_of(mc * half, half), half), :], ref[...], preferred_element_type=F32
            )
            for k, (part, h) in enumerate(pieces):
                v = prod[:, k * 128 : (k + 1) * 128]
                if part < 2:
                    v = normed(v, (qg if part == 0 else kg)[h : h + 1, :])
                v = v.reshape(frames, 2, 8, 2, 8, 128)
                at = pl.ds(pl.multiple_of(mc * 64 * frames, 64), 64 * frames)
                for i in range(2):
                    for j in range(2):
                        tile = v[:, i, :, j].reshape(64 * frames, 128).astype(BF)
                        if part == 0:
                            qb[h, i * 2 + j, at, :] = tile
                        else:
                            nb[h][1 + j, part - 1, 2 * t + i, at, :] = tile
            return carry

        lax.fori_loop(0, 6 // frames, step, 0)
    def text_product(g):
        ref, h = wv[g], GROUP_PIECES[g][0][1]
        prod = jnp.dot(tv[...], ref[...], preferred_element_type=F32)
        tkv[h, 0] = normed(prod[:, :128], kg[h : h + 1, :]).astype(BF)
        tkv[h, 1] = prod[:, 128:].astype(BF)

    near, far, relays, cores = [None] * 3, [None] * 3, [[], [], []], [None] * 3

    def near_post(h):
        b = nb[h]
        near[h] = (
            (mail.post(b.at[1, :, mine], b.at[3, :, mine], "left"), b.at[3, :, mine]),
            (mail.post(b.at[2, :, mine], b.at[0, :, mine], "right"), b.at[0, :, mine]),
        )
        cores[h] = mail.post(b.at[pl.ds(1, 2), :, mine], b.at[pl.ds(1, 2), :, mine], "core")

    def far_post(h):
        b, f = nb[h], fb[h]
        far[h] = (
            (mail.post(b.at[2, :, mine], f.at[1, :, mine], "left"), f.at[1, :, mine]),
            (mail.post(b.at[1, :, mine], f.at[0, :, mine], "right"), f.at[0, :, mine]),
        )

    def relay(copies):
        passed = []
        for cp, ref in copies:
            cp.wait_recv()
            passed.append(mail.post(ref, ref, "core"))
        return passed

    def await_all(copies):
        for cp in copies:
            cp.wait_recv()

    count = cnt[0]

    def window(h, k):
        i, j = k // 2, lax.rem(k, 2)
        row = jnp.clip(2 * t + i + off[0, h], 1, 2) - 1
        col = jnp.clip(2 * w + j + off[1, h], 1, 6) + 1 - 2 * w
        return row, col, j

    def near_attend(h):
        await_all([cores[h]])

        def tile(k, carry):
            row, col, j = window(h, k)
            q = qb[h, k]
            p = weights_of(q, tkv[h, 0])
            p = jnp.where(lax.broadcasted_iota(jnp.int32, p.shape, 1) < count, p, 0.0)
            den = jnp.sum(p, axis=1, keepdims=True)
            acc = jnp.dot(p.astype(BF), tkv[h, 1], preferred_element_type=F32)
            for d in range(2):
                p = weights_of(q, nb[h][col - j + d, 0, pl.ds(row, 3)].reshape(3 * TILE, 128))
                den = den + jnp.sum(p, axis=1, keepdims=True)
                v = nb[h][col - j + d, 1, pl.ds(row, 3)].reshape(3 * TILE, 128)
                acc = acc + jnp.dot(p.astype(BF), v, preferred_element_type=F32)
            acc_s[h, k] = acc
            den_s[h, k] = jnp.broadcast_to(den, (TILE, 128))
            return carry

        lax.fori_loop(0, 4, tile, 0)

    sends = [None] * 3

    def far_tile(h, k, part=slice(0, TILE)):
        row, col, j = window(h, k)
        last = col + 2 * j
        is_far = jnp.logical_or(last == 0, last == 5)
        at = jnp.clip(last - 1, 0, 3)

        def pick(kind):
            a = fb[h][j, kind, pl.ds(row, 3)].reshape(3 * TILE, 128)
            b = nb[h][at, kind, pl.ds(row, 3)].reshape(3 * TILE, 128)
            return jnp.where(is_far, a, b)

        p = weights_of(qb[h, k, part, :], pick(0))
        den = den_s[h, k, part, :] + jnp.sum(p, axis=1, keepdims=True)
        acc = acc_s[h, k, part, :] + jnp.dot(p.astype(BF), pick(1), preferred_element_type=F32)
        return (acc / den).astype(BF)

    def far_attend(h, runs=1):
        def tile(n, carry):
            cc = c + (1 - 2 * c) * (1 - lax.rem(n, 2))
            xx = x + (1 - 2 * x) * (1 - n // 2)
            att[h, cc * 2 + xx] = far_tile(h, cc * 2 + xx)
            return carry

        sends[h] = []
        for n in range(runs):
            lax.fori_loop(n * 4 // runs, (n + 1) * 4 // runs, tile, 0)
            for name, cc, xx in peers[n * 4 // runs : (n + 1) * 4 // runs]:
                sends[h].append(mail.post(att.at[h, cc * 2 + xx], box.at[h, spot], name))
        box[h, spot] = att[h, spot]

    y_got = [None] * 3
    gs = guide[0]
    y_lane = pl.ds(pl.multiple_of(y * 128, 128), 128)

    def mix(h, a=0, pieces=1):
        part = slice(a * (TILE // pieces), (a + 1) * (TILE // pieces))
        if a == 0:
            await_all(sends[h])
        for xx in range(2):
            mixed = gs * box[h, xx, part, :].astype(F32) + (1.0 - gs) * box[h, 2 + xx, part, :].astype(F32)
            comb[h, xx, part, :] = mixed.astype(BF)
        src = comb.at[h, :, part]
        y_got[h] = [mail.post(src, cb.at[h, :, part, y_lane], name) for name in ("yfar", "up", "down")]
        for xx in range(2):
            cb[h, xx, part, y_lane] = comb[h, xx, part, :]
        return y_got[h]

    def term(h, cc, xx, part=slice(0, TILE)):
        total = None
        for k in range(2):
            prod = lax.dot_general(
                cb[h, k, part, :], wt[h, k, cc, xx], (((1,), (1,)), ((), ())), preferred_element_type=F32
            )
            total = prod if total is None else total + prod
        return total

    def early_product(h):
        await_all(y_got[h])

        def dest(d, carry):
            cc, xx = d // 2, lax.rem(d, 2)
            if h == 0:
                oacc[d] = term(h, cc, xx)
            else:
                oacc[d] += term(h, cc, xx)
            return carry

        lax.fori_loop(0, 4, dest, 0)

    start_own(0, ("left", "right", "xl", "core"))
    start_own(1, ("left", "right", "xl", "core"))
    o_left = mail.post(woz.at[w], woz.at[w], "left")
    o_right = mail.post(woz.at[w], woz.at[w], "right")
    z_near(0)
    x_near(0)
    start_own(2, ("left", "right", "core", "xl"))
    z_far(0)
    z_near(1)
    x_side(0)
    start_own(3, ("left", "right", "core"))
    start_own(4, ("left", "right", "core"))
    z_far(1)
    o_right.wait_recv()
    o_r2 = mail.post(woz.at[wl, :, pl.ds(0, 96)], woz.at[wl, :, pl.ds(0, 96)], "right")
    o_left.wait_recv()
    o_l2 = mail.post(woz.at[wr, :, pl.ds(96, 96)], woz.at[wr, :, pl.ds(96, 96)], "left")
    z_near(2)
    z_far(2)
    start_own(3, ("xl",))
    x_far(0)
    z_near(3)
    start_own(4, ("xl",))
    z_near(4)
    for cp in loads:
        cp.wait()
    multiply(0)
    near_post(0)
    far_post(0)
    z_far(3)
    z_far(4)
    text_product(0)
    o_r2.wait_recv()
    o_l2.wait_recv()
    o_y = []
    for name, yy in (("up", lax.rem(y + 1, 4)), ("down", lax.rem(y + 3, 4)), ("yfar", lax.rem(y + 2, 4))):
        o_y.append(mail.post(woz.at[yy], woy.at[:, :, y_lane], name))
    woy[:, :, y_lane] = woz[y]
    x_events(1)
    multiply(1)
    near_post(1)
    far_post(1)
    text_product(1)
    x_events(2)
    multiply(2)
    await_all(o_y)
    o_xl, o_xd, o_xf, o_core = [None] * 3, [None] * 3, [None] * 3, [[], [], []]
    for h in range(3):
        o_xl[h] = mail.post(woy.at[h], wt.at[h, x, c, t], "xl")
        o_xd[h] = mail.post(woy.at[h], wt.at[h, x, c, t], "xd")
        o_core[h].append(mail.post(woy.at[h], wt.at[h, x, c, t], "core"))

    def o_cross(h):
        o_xl[h].wait_recv()
        at = wt.at[h, x, 1 - c, t]
        o_core[h].append(mail.post(at, at, "core"))
        o_xf[h] = mail.post(at, at, "xd")
        o_xd[h].wait_recv()
        at = wt.at[h, 1 - x, 1 - c, t]
        o_core[h].append(mail.post(at, at, "core"))

    def o_last(h):
        o_xf[h].wait_recv()
        at = wt.at[h, 1 - x, c, t]
        o_core[h].append(mail.post(at, at, "core"))

    o_keep = pltpu.make_async_copy(woy, wt.at[:, x, c, t], lsem.at[3])
    o_keep.start()
    relays[0] += relay(near[0])
    x_events(3)
    multiply(3)
    near_post(2)
    far_post(2)
    text_product(3)
    await_all(relays[0])
    near_attend(0)
    tail = relay(far[0])
    await_all(tail)
    far_attend(0)
    x_events(4)
    multiply(4)
    relays[1] += relay(near[1])
    await_all(relays[1])
    o_cross(0)
    near_attend(1)
    tail = relay(far[1])
    mix(0)
    o_cross(1)
    await_all(tail)
    far_attend(1)
    o_cross(2)
    relays[2] += relay(near[2])
    await_all(relays[2])
    near_attend(2)
    mix(1)
    tail = relay(far[2])
    await_all(tail)
    far_attend(2, 2)
    o_keep.wait()
    for h in range(3):
        o_last(h)
    await_all(o_core[0])
    early_product(0)
    await_all(o_core[1])
    early_product(1)
    await_all(o_core[2])
    y_parts = [mix(2, a, PIECES) for a in range(PIECES)]
    last = []
    for a in range(PIECES):
        part = slice(a * (TILE // PIECES), (a + 1) * (TILE // PIECES))
        await_all(y_parts[a])
        for n, (name, cc, xx) in enumerate(peers):
            mid[n, part, :] = (oacc[cc * 2 + xx, part, :] + term(2, cc, xx, part)).astype(BF)
            last.append(mail.post(mid.at[n, part], ends.at[spot, part], name))
        ends[spot, part, :] = (oacc[spot, part, :] + term(2, c, x, part)).astype(BF)
    await_all(last)
    for i in range(2):
        sides = [ends[i * 2 + j].astype(F32).reshape(6, 8, 8, 192) for j in range(2)]
        out[:, i * 8 : (i + 1) * 8] = jnp.concatenate(sides, axis=2).astype(BF)
    mail.close()


def sublayer(video, wq, wo, text, qg, kg, off, cnt, guide):
    near = pltpu.VMEM((4, 2, 4, TILE, 128), BF)
    far = pltpu.VMEM((2, 2, 4, TILE, 128), BF)
    return pl.pallas_call(
        sublayer_kernel,
        out_shape=jax.ShapeDtypeStruct((6, 16, 16, 192), BF),
        in_specs=[ANY, ANY, ANY, ANY, VMEM, VMEM, SMEM, SMEM, SMEM],
        out_specs=VMEM,
        scratch_shapes=[
            pltpu.VMEM((TOK, 3072), BF),
            pltpu.VMEM((256, 3072), BF),
            pltpu.VMEM((3072, 256), BF),
            pltpu.VMEM((3072, 256), BF),
            pltpu.VMEM((3072, 256), BF),
            pltpu.VMEM((3072, 256), BF),
            pltpu.VMEM((3072, 128), BF),
            pltpu.VMEM((4, 3, 192, 128), BF),
            pltpu.VMEM((3, 192, 512), BF),
            pltpu.VMEM((3, 2, 2, 2, 192, 512), BF),
            pltpu.VMEM((3, 4, TILE, 128), BF),
            pltpu.VMEM((3, 2, 256, 128), BF),
            near,
            near,
            near,
            far,
            far,
            far,
            pltpu.VMEM((3, 4, TILE, 128), F32),
            pltpu.VMEM((3, 4, TILE, 128), F32),
            pltpu.VMEM((3, 4, TILE, 128), BF),
            pltpu.VMEM((3, 4, TILE, 128), BF),
            pltpu.VMEM((3, 2, TILE, 128), BF),
            pltpu.VMEM((3, 2, TILE, 512), BF),
            pltpu.VMEM((4, TILE, 192), F32),
            pltpu.VMEM((3, TILE, 192), BF),
            pltpu.VMEM((4, TILE, 192), BF),
            pltpu.SemaphoreType.DMA((20,)),
            pltpu.SemaphoreType.DMA((N_MAIL,)),
            pltpu.SemaphoreType.DMA((N_MAIL,)),
        ],
        compiler_params=pltpu.CompilerParams(collective_id=0, has_side_effects=True, vmem_limit_bytes=LIMIT),
    )(video, wq, wo, text, qg, kg, off, cnt, guide)


def body(video, text_states, text_count, guidance, window_offsets, w_qkv, q_gain, k_gain, w_out):
    return sublayer(
        video.reshape(TOK, 3072),
        w_qkv.swapaxes(0, 1),
        w_out.T,
        text_states[0],
        q_gain,
        k_gain,
        window_offsets.T,
        text_count,
        guidance,
    )


def solution(mesh):
    return jax.shard_map(
        body,
        mesh=mesh,
        in_specs=(
            P("cfg", None, "th", "tw", None),
            P("cfg", None, None),
            P("cfg"),
            P(),
            P("hd", None),
            P(("cfg", "th", "tw"), None, "hd"),
            P("hd", None),
            P("hd", None),
            P("hd", ("cfg", "th", "tw")),
        ),
        out_specs=P(None, "th", "tw", ("cfg", "hd")),
        check_vma=False,
    )
```

```python
import functools
import math

import jax
import jax.numpy as jnp
from jax import lax
from jax.experimental import pallas as pl
from jax.experimental.pallas import tpu as pltpu
from jax.sharding import PartitionSpec as P

MESH = pl.DeviceIdType.MESH
BF = jnp.bfloat16
F32 = jnp.float32
VMEM = pl.BlockSpec(memory_space=pltpu.VMEM)
SMEM = pl.BlockSpec(memory_space=pltpu.SMEM)
ANY = pl.BlockSpec(memory_space=pl.ANY)
LIMIT = 62 << 20
TILE = 384
TOK = 1536


def place():
    c, t, w, h = (lax.axis_index(a) for a in ("cfg", "th", "tw", "hd"))
    return c, t, w, h // 4, lax.rem(h, 4)


def partners():
    c, t, w, x, y = place()
    return {
        "left": {"tw": lax.rem(w + 3, 4)},
        "right": {"tw": lax.rem(w + 1, 4)},
        "core": {"th": 1 - t},
        "xl": {"cfg": 1 - c},
        "xh": {"hd": (1 - x) * 4 + y},
        "xd": {"cfg": 1 - c, "hd": (1 - x) * 4 + y},
        "up": {"hd": x * 4 + lax.rem(y + 1, 4)},
        "down": {"hd": x * 4 + lax.rem(y + 3, 4)},
        "yfar": {"hd": x * 4 + lax.rem(y + 2, 4)},
    }


def greet(names):
    to = partners()
    barrier = pltpu.get_barrier_semaphore()
    for name in names:
        pl.semaphore_signal(barrier, inc=1, device_id=to[name], device_id_type=MESH)
    pl.semaphore_wait(barrier, len(names))


class Mail:
    def __init__(self, send, recv):
        self.send, self.recv, self.n, self.all = send, recv, 0, []
        self.to = partners()

    def copy(self, src, dst, name):
        k = self.n
        self.n += 1
        cp = pltpu.make_async_remote_copy(
            src_ref=src,
            dst_ref=dst,
            send_sem=self.send.at[k],
            recv_sem=self.recv.at[k],
            device_id=self.to[name],
            device_id_type=MESH,
        )
        self.all.append(cp)
        return cp

    def post(self, src, dst, name):
        cp = self.copy(src, dst, name)
        cp.start()
        return cp

    def close(self):
        for cp in self.all:
            cp.wait_send()


def normed(v, gain):
    ms = jnp.mean(v * v, axis=-1, keepdims=True)
    return v * lax.rsqrt(ms + 1e-06) * gain


SCALE = math.log2(math.e) / math.sqrt(128.0)


def weights_of(q, keys):
    s = lax.dot_general(q, keys, (((1,), (1,)), ((), ())), preferred_element_type=F32)
    return jnp.exp2(s * SCALE)


GROUP_PIECES = (((1, 0), (2, 0)), ((1, 1), (2, 1)), ((0, 0), (0, 1)), ((1, 2), (2, 2)), ((0, 2),))
N_GROUPS = len(GROUP_PIECES)
BY_Z = (0,)
FRAMES = 3
PIECES = 4
N_MAIL = 224
EVERYONE = ("left", "right", "core", "xl", "xh", "xd", "up", "down", "yfar")


def sublayer_kernel(
    video, wq, wo, text, qg, kg, off, cnt, guide, out,
    xv, tv, wv0, wv1, wv2, wv3, wv4, woz, woy, wt, qb, tkv, nb0, nb1, nb2, fb0, fb1, fb2, acc_s, den_s,
    att, box, comb, cb, oacc, mid, ends, lsem, ssem, rsem,
):
    c, t, w, x, y = place()
    wv = (wv0, wv1, wv2, wv3, wv4)
    nb = (nb0, nb1, nb2)
    fb = (fb0, fb1, fb2)
    half = 768
    mine = pl.ds(2 * t, 2)
    spot = c * 2 + x
    peers = (("xd", 1 - c, 1 - x), ("xh", c, 1 - x), ("xl", 1 - c, x))

    def rows(cc, tt, ww):
        return pl.ds(pl.multiple_of((cc * 8 + tt * 4 + ww) * 192, 64), 192)

    def half_rows(cc, tt, ww, k):
        return pl.ds(pl.multiple_of((cc * 8 + tt * 4 + ww) * 192 + k * 96, 32), 96)

    own = rows(c, t, w)
    w_loads = []
    n = 4
    for g, pieces in enumerate(GROUP_PIECES):
        for k, (part, h) in enumerate(pieces):
            cp = pltpu.make_async_copy(
                wq.at[part, :, pl.ds(h * 128, 128)], wv[g].at[own, pl.ds(k * 128, 128)], lsem.at[n]
            )
            n += 1
            cp.start()
            w_loads.append(cp)
    for h in range(3):
        cp = pltpu.make_async_copy(wo.at[:, pl.ds(h * 128, 128)], woz.at[w, h], lsem.at[n])
        n += 1
        cp.start()
        w_loads.append(cp)
    loads = [
        pltpu.make_async_copy(video.at[pl.ds(i * half, half)], xv.at[pl.ds(i * half, half)], lsem.at[i])
        for i in range(2)
    ]
    loads.append(pltpu.make_async_copy(text, tv, lsem.at[2]))
    for cp in loads:
        cp.start()
    greet(EVERYONE)
    for cp in w_loads:
        cp.wait()
    mail = Mail(ssem, rsem)
    wl, wr, w2 = lax.rem(w + 3, 4), lax.rem(w + 1, 4), lax.rem(w + 2, 4)
    state = [{} for _ in range(N_GROUPS)]

    def start_own(g, names):
        for name in names:
            state[g][name] = mail.post(wv[g].at[own], wv[g].at[own], name)

    def pass_on(g, key, r, names):
        for tag, name in names:
            state[g][tag] = mail.post(wv[g].at[r], wv[g].at[r], name)

    def z_near(g):
        s = state[g]
        s["right"].wait_recv()
        pass_on(g, "r2", half_rows(c, t, wl, 0), [("r2", "right")])
        pass_on(g, "c1", rows(c, t, wl), [("c1", "core")] + ([] if g in BY_Z else [("x1", "xl")]))
        s["left"].wait_recv()
        pass_on(g, "l2", half_rows(c, t, wr, 1), [("l2", "left")])
        pass_on(g, "c2", rows(c, t, wr), [("c2", "core")] + ([] if g in BY_Z else [("x2", "xl")]))

    def z_far(g):
        s = state[g]
        s["r2"].wait_recv()
        s["l2"].wait_recv()
        pass_on(g, "x3", rows(c, t, w2), [("x3", "xl"), ("c3", "core")])

    def x_near(g):
        state[g]["xl"].wait_recv()
        names = [("d0", "core")]
        if g in BY_Z:
            names = [("x1", "right"), ("x2", "left")] + names
        pass_on(g, "d0", rows(1 - c, t, w), names)

    def x_side(g):
        state[g]["x1"].wait_recv()
        pass_on(g, "d1", rows(1 - c, t, wl), [("d1", "core")])
        state[g]["x2"].wait_recv()
        pass_on(g, "d2", rows(1 - c, t, wr), [("d2", "core")])

    def x_far(g):
        s = state[g]
        s["x3"].wait_recv()
        pass_on(g, "d3", rows(1 - c, t, w2), [("d3", "core")])
        for key in ("core", "c1", "c2", "c3", "d0", "d1", "d2", "d3"):
            s[key].wait_recv()

    def x_events(g):
        x_near(g)
        x_side(g)
        x_far(g)

    def multiply(g):
        ref, pieces = wv[g], GROUP_PIECES[g]

        frames = FRAMES
        half = 256 * frames

        def step(mc, carry):
            prod = jnp.dot(
                xv[pl.ds(pl.multiple_of(mc * half, half), half), :], ref[...], preferred_element_type=F32
            )
            for k, (part, h) in enumerate(pieces):
                v = prod[:, k * 128 : (k + 1) * 128]
                if part < 2:
                    v = normed(v, (qg if part == 0 else kg)[h : h + 1, :])
                v = v.reshape(frames, 2, 8, 2, 8, 128)
                at = pl.ds(pl.multiple_of(mc * 64 * frames, 64), 64 * frames)
                for i in range(2):
                    for j in range(2):
                        tile = v[:, i, :, j].reshape(64 * frames, 128).astype(BF)
                        if part == 0:
                            qb[h, i * 2 + j, at, :] = tile
                        else:
                            nb[h][1 + j, part - 1, 2 * t + i, at, :] = tile
            return carry

        lax.fori_loop(0, 6 // frames, step, 0)
    def text_product(g):
        ref, h = wv[g], GROUP_PIECES[g][0][1]
        prod = jnp.dot(tv[...], ref[...], preferred_element_type=F32)
        tkv[h, 0] = normed(prod[:, :128], kg[h : h + 1, :]).astype(BF)
        tkv[h, 1] = prod[:, 128:].astype(BF)

    near, far, relays, cores = [None] * 3, [None] * 3, [[], [], []], [None] * 3

    def near_post(h):
        b = nb[h]
        near[h] = (
            (mail.post(b.at[1, :, mine], b.at[3, :, mine], "left"), b.at[3, :, mine]),
            (mail.post(b.at[2, :, mine], b.at[0, :, mine], "right"), b.at[0, :, mine]),
        )
        cores[h] = mail.post(b.at[pl.ds(1, 2), :, mine], b.at[pl.ds(1, 2), :, mine], "core")

    def far_post(h):
        b, f = nb[h], fb[h]
        far[h] = (
            (mail.post(b.at[2, :, mine], f.at[1, :, mine], "left"), f.at[1, :, mine]),
            (mail.post(b.at[1, :, mine], f.at[0, :, mine], "right"), f.at[0, :, mine]),
        )

    def relay(copies):
        passed = []
        for cp, ref in copies:
            cp.wait_recv()
            passed.append(mail.post(ref, ref, "core"))
        return passed

    def await_all(copies):
        for cp in copies:
            cp.wait_recv()

    count = cnt[0]

    def window(h, k):
        i, j = k // 2, lax.rem(k, 2)
        row = jnp.clip(2 * t + i + off[0, h], 1, 2) - 1
        col = jnp.clip(2 * w + j + off[1, h], 1, 6) + 1 - 2 * w
        return row, col, j

    def near_attend(h):
        await_all([cores[h]])

        def tile(k, carry):
            row, col, j = window(h, k)
            q = qb[h, k]
            p = weights_of(q, tkv[h, 0])
            p = jnp.where(lax.broadcasted_iota(jnp.int32, p.shape, 1) < count, p, 0.0)
            den = jnp.sum(p, axis=1, keepdims=True)
            acc = jnp.dot(p.astype(BF), tkv[h, 1], preferred_element_type=F32)
            for d in range(2):
                p = weights_of(q, nb[h][col - j + d, 0, pl.ds(row, 3)].reshape(3 * TILE, 128))
                den = den + jnp.sum(p, axis=1, keepdims=True)
                v = nb[h][col - j + d, 1, pl.ds(row, 3)].reshape(3 * TILE, 128)
                acc = acc + jnp.dot(p.astype(BF), v, preferred_element_type=F32)
            acc_s[h, k] = acc
            den_s[h, k] = jnp.broadcast_to(den, (TILE, 128))
            return carry

        lax.fori_loop(0, 4, tile, 0)

    sends = [None] * 3

    def far_tile(h, k, part=slice(0, TILE)):
        row, col, j = window(h, k)
        last = col + 2 * j
        is_far = jnp.logical_or(last == 0, last == 5)
        at = jnp.clip(last - 1, 0, 3)

        def pick(kind):
            a = fb[h][j, kind, pl.ds(row, 3)].reshape(3 * TILE, 128)
            b = nb[h][at, kind, pl.ds(row, 3)].reshape(3 * TILE, 128)
            return jnp.where(is_far, a, b)

        p = weights_of(qb[h, k, part, :], pick(0))
        den = den_s[h, k, part, :] + jnp.sum(p, axis=1, keepdims=True)
        acc = acc_s[h, k, part, :] + jnp.dot(p.astype(BF), pick(1), preferred_element_type=F32)
        return (acc / den).astype(BF)

    def far_attend(h, runs=1):
        def tile(n, carry):
            cc = c + (1 - 2 * c) * (1 - lax.rem(n, 2))
            xx = x + (1 - 2 * x) * (1 - n // 2)
            att[h, cc * 2 + xx] = far_tile(h, cc * 2 + xx)
            return carry

        sends[h] = []
        for n in range(runs):
            lax.fori_loop(n * 4 // runs, (n + 1) * 4 // runs, tile, 0)
            for name, cc, xx in peers[n * 4 // runs : (n + 1) * 4 // runs]:
                sends[h].append(mail.post(att.at[h, cc * 2 + xx], box.at[h, spot], name))
        box[h, spot] = att[h, spot]

    y_got = [None] * 3
    gs = guide[0]
    y_lane = pl.ds(pl.multiple_of(y * 128, 128), 128)

    def mix(h, a=0, pieces=1):
        part = slice(a * (TILE // pieces), (a + 1) * (TILE // pieces))
        if a == 0:
            await_all(sends[h])
        for xx in range(2):
            mixed = gs * box[h, xx, part, :].astype(F32) + (1.0 - gs) * box[h, 2 + xx, part, :].astype(F32)
            comb[h, xx, part, :] = mixed.astype(BF)
        src = comb.at[h, :, part]
        y_got[h] = [mail.post(src, cb.at[h, :, part, y_lane], name) for name in ("up", "down", "yfar")]
        for xx in range(2):
            cb[h, xx, part, y_lane] = comb[h, xx, part, :]
        return y_got[h]

    def term(h, cc, xx, part=slice(0, TILE)):
        total = None
        for k in range(2):
            prod = lax.dot_general(
                cb[h, k, part, :], wt[h, k, cc, xx], (((1,), (1,)), ((), ())), preferred_element_type=F32
            )
            total = prod if total is None else total + prod
        return total

    def early_product(h):
        await_all(y_got[h])

        def dest(d, carry):
            cc, xx = d // 2, lax.rem(d, 2)
            if h == 0:
                oacc[d] = term(h, cc, xx)
            else:
                oacc[d] += term(h, cc, xx)
            return carry

        lax.fori_loop(0, 4, dest, 0)

    start_own(0, ("left", "right", "xl", "core"))
    start_own(1, ("left", "right", "xl", "core"))
    o_left = mail.post(woz.at[w], woz.at[w], "left")
    o_right = mail.post(woz.at[w], woz.at[w], "right")
    z_near(0)
    x_near(0)
    start_own(2, ("left", "right", "core", "xl"))
    z_far(0)
    z_near(1)
    x_side(0)
    start_own(3, ("left", "right", "core"))
    start_own(4, ("left", "right", "core"))
    z_far(1)
    o_right.wait_recv()
    o_r2 = mail.post(woz.at[wl, :, pl.ds(0, 96)], woz.at[wl, :, pl.ds(0, 96)], "right")
    o_left.wait_recv()
    o_l2 = mail.post(woz.at[wr, :, pl.ds(96, 96)], woz.at[wr, :, pl.ds(96, 96)], "left")
    z_near(2)
    z_far(2)
    start_own(3, ("xl",))
    x_far(0)
    z_near(3)
    start_own(4, ("xl",))
    z_near(4)
    for cp in loads:
        cp.wait()
    multiply(0)
    near_post(0)
    far_post(0)
    z_far(3)
    z_far(4)
    text_product(0)
    o_r2.wait_recv()
    o_l2.wait_recv()
    o_y = []
    for name, yy in (("up", lax.rem(y + 1, 4)), ("down", lax.rem(y + 3, 4)), ("yfar", lax.rem(y + 2, 4))):
        o_y.append(mail.post(woz.at[yy], woy.at[:, :, y_lane], name))
    woy[:, :, y_lane] = woz[y]
    x_events(1)
    multiply(1)
    near_post(1)
    far_post(1)
    text_product(1)
    x_events(2)
    multiply(2)
    await_all(o_y)
    o_xl, o_xd, o_xf, o_core = [None] * 3, [None] * 3, [None] * 3, [[], [], []]
    for h in range(3):
        o_xl[h] = mail.post(woy.at[h], wt.at[h, x, c, t], "xl")
        o_xd[h] = mail.post(woy.at[h], wt.at[h, x, c, t], "xd")
        o_core[h].append(mail.post(woy.at[h], wt.at[h, x, c, t], "core"))

    def o_cross(h):
        o_xl[h].wait_recv()
        at = wt.at[h, x, 1 - c, t]
        o_core[h].append(mail.post(at, at, "core"))
        o_xf[h] = mail.post(at, at, "xd")
        o_xd[h].wait_recv()
        at = wt.at[h, 1 - x, 1 - c, t]
        o_core[h].append(mail.post(at, at, "core"))

    def o_last(h):
        o_xf[h].wait_recv()
        at = wt.at[h, 1 - x, c, t]
        o_core[h].append(mail.post(at, at, "core"))

    o_keep = pltpu.make_async_copy(woy, wt.at[:, x, c, t], lsem.at[3])
    o_keep.start()
    relays[0] += relay(near[0])
    x_events(3)
    multiply(3)
    near_post(2)
    far_post(2)
    text_product(3)
    await_all(relays[0])
    near_attend(0)
    x_events(4)
    multiply(4)
    tail = relay(far[0])
    await_all(tail)
    far_attend(0)
    relays[1] += relay(near[1])
    await_all(relays[1])
    o_cross(0)
    near_attend(1)
    tail = relay(far[1])
    mix(0)
    o_cross(1)
    await_all(tail)
    far_attend(1)
    o_cross(2)
    relays[2] += relay(near[2])
    await_all(relays[2])
    near_attend(2)
    mix(1)
    tail = relay(far[2])
    await_all(tail)
    far_attend(2, 2)
    o_keep.wait()
    for h in range(3):
        o_last(h)
    await_all(o_core[0])
    early_product(0)
    y_parts = [mix(2, a, PIECES) for a in range(PIECES)]
    await_all(o_core[1])
    early_product(1)
    await_all(o_core[2])
    last = []
    for a in range(PIECES):
        part = slice(a * (TILE // PIECES), (a + 1) * (TILE // PIECES))
        await_all(y_parts[a])
        for n, (name, cc, xx) in enumerate(peers):
            mid[n, part, :] = (oacc[cc * 2 + xx, part, :] + term(2, cc, xx, part)).astype(BF)
            last.append(mail.post(mid.at[n, part], ends.at[spot, part], name))
        ends[spot, part, :] = (oacc[spot, part, :] + term(2, c, x, part)).astype(BF)
    await_all(last)
    for i in range(2):
        sides = [ends[i * 2 + j].astype(F32).reshape(6, 8, 8, 192) for j in range(2)]
        out[:, i * 8 : (i + 1) * 8] = jnp.concatenate(sides, axis=2).astype(BF)
    mail.close()


def sublayer(video, wq, wo, text, qg, kg, off, cnt, guide):
    near = pltpu.VMEM((4, 2, 4, TILE, 128), BF)
    far = pltpu.VMEM((2, 2, 4, TILE, 128), BF)
    return pl.pallas_call(
        sublayer_kernel,
        out_shape=jax.ShapeDtypeStruct((6, 16, 16, 192), BF),
        in_specs=[ANY, ANY, ANY, ANY, VMEM, VMEM, SMEM, SMEM, SMEM],
        out_specs=VMEM,
        scratch_shapes=[
            pltpu.VMEM((TOK, 3072), BF),
            pltpu.VMEM((256, 3072), BF),
            pltpu.VMEM((3072, 256), BF),
            pltpu.VMEM((3072, 256), BF),
            pltpu.VMEM((3072, 256), BF),
            pltpu.VMEM((3072, 256), BF),
            pltpu.VMEM((3072, 128), BF),
            pltpu.VMEM((4, 3, 192, 128), BF),
            pltpu.VMEM((3, 192, 512), BF),
            pltpu.VMEM((3, 2, 2, 2, 192, 512), BF),
            pltpu.VMEM((3, 4, TILE, 128), BF),
            pltpu.VMEM((3, 2, 256, 128), BF),
            near,
            near,
            near,
            far,
            far,
            far,
            pltpu.VMEM((3, 4, TILE, 128), F32),
            pltpu.VMEM((3, 4, TILE, 128), F32),
            pltpu.VMEM((3, 4, TILE, 128), BF),
            pltpu.VMEM((3, 4, TILE, 128), BF),
            pltpu.VMEM((3, 2, TILE, 128), BF),
            pltpu.VMEM((3, 2, TILE, 512), BF),
            pltpu.VMEM((4, TILE, 192), F32),
            pltpu.VMEM((3, TILE, 192), BF),
            pltpu.VMEM((4, TILE, 192), BF),
            pltpu.SemaphoreType.DMA((20,)),
            pltpu.SemaphoreType.DMA((N_MAIL,)),
            pltpu.SemaphoreType.DMA((N_MAIL,)),
        ],
        compiler_params=pltpu.CompilerParams(collective_id=0, has_side_effects=True, vmem_limit_bytes=LIMIT),
    )(video, wq, wo, text, qg, kg, off, cnt, guide)


def body(video, text_states, text_count, guidance, window_offsets, w_qkv, q_gain, k_gain, w_out):
    return sublayer(
        video.reshape(TOK, 3072),
        w_qkv.swapaxes(0, 1),
        w_out.T,
        text_states[0],
        q_gain,
        k_gain,
        window_offsets.T,
        text_count,
        guidance,
    )


def solution(mesh):
    return jax.shard_map(
        body,
        mesh=mesh,
        in_specs=(
            P("cfg", None, "th", "tw", None),
            P("cfg", None, None),
            P("cfg"),
            P(),
            P("hd", None),
            P(("cfg", "th", "tw"), None, "hd"),
            P("hd", None),
            P("hd", None),
            P("hd", ("cfg", "th", "tw")),
        ),
        out_specs=P(None, "th", "tw", ("cfg", "hd")),
        check_vma=False,
    )
```
